128 devices in a mesh: expert: 64 (over z, y, x_hi, core), dp: 2 (over x_lo).
Axes of the slice: x: 4 (x_hi: 2, x_lo: 2; x = x_hi * 2 + x_lo), y: 4, z: 4, core: 2. Of those that a mesh axis runs over, the one named last changes fastest.
Arguments:
- activations: bfloat16 [16384, 3584], P(('expert', 'dp')), may hold values from -6 to 6
- out_grad: bfloat16 [16384, 3584], P(('expert', 'dp')), may hold values from -1.5 to 1.5
- expert_ids: int32 [16384, 1], P(('expert', 'dp')), may hold values from 0 to 63; in each aligned block of 128 rows (0 to 127, 128 to 255, ...) at most 6 rows name the same one
- gate_probs: bfloat16 [16384, 1], P(('expert', 'dp')), may hold values from 0.049804688 to 1
- gate_weight: bfloat16 [64, 3584, 1024], P('expert', 'dp'), may hold values from -0.09375 to 0.09375
- up_weight: bfloat16 [64, 3584, 1024], P('expert', 'dp'), may hold values from -0.09375 to 0.09375
- down_weight: bfloat16 [64, 3584, 1024], P('expert', 'dp'), may hold values from -0.1875 to 0.1875
Outputs:
- input_delta: bfloat16 [16384, 3584], P(('expert', 'dp'))
- prob_delta: bfloat16 [16384, 1], P(('expert', 'dp'))
- gate_delta: bfloat16 [64, 3584, 1024], P('expert', 'dp')
- up_delta: bfloat16 [64, 3584, 1024], P('expert', 'dp')
- down_delta: bfloat16 [64, 3584, 1024], P('expert', 'dp')
The draws below stay inside these ranges and needn't reach their ends.
Inputs may be any that keep to these rules, and one draw needn't show every extreme that they name: `expert_ids`: among the 128 tokens of one device (aligned blocks of rows), no expert is named more than 6 times, a bound that some block reaches.
All inputs are finite; a program needn't handle non-finite values.
Results may differ from the reference program's by a relative error of at most 0.034.
Values may be sent and summed in bfloat16 or wider, within the bound.
A program may use at most 128 MiB of HBM per device.

```python
import math
import jax
import jax.numpy as jnp
import numpy as np
from jax import lax

D = 3584
F = 1024
TOP = 1
TOK_DEV = 128
EXPERTS = 64
CAP = 6
TOKENS = 16384
N_EXPERT = 64
N_DP = 2


def steps_of(own_key, shape, cuts, low, high):
    def one(position, blocks):
        steps = jax.random.uniform(jax.random.fold_in(jax.random.fold_in(own_key, 6), position), (blocks,), jnp.float32, low / len(cuts), high / len(cuts))
        return jnp.repeat(jnp.exp(steps), shape[position] // blocks).reshape((-1,) + (1,) * (len(shape) - position - 1))

    factor_of = one(*cuts[0])
    for cut in cuts[1:]:
        factor_of = factor_of * one(*cut)
    return factor_of


def assign_block(key, own, number, rows, amount, top, limit, skew):
    order = jax.random.permutation(key, amount)
    heavy_load, common = load_shares(amount, rows * top, limit, skew, True), load_shares(amount, rows * top, limit, skew, False)
    places = jnp.arange(amount)

    def named(lengths, turn):
        used = int((lengths > 0).sum())
        fixed = max(1, used // 4)
        passed = fixed + (places - fixed + turn * (used - fixed)) % max(1, amount - fixed)
        return jnp.zeros((amount,), jnp.int32).at[order[jnp.where(places < fixed, places, passed)]].set(jnp.asarray(lengths, jnp.int32))

    lengths = jnp.where(number % 4 == 0, named(heavy_load, number // 4), named(common, number - number // 4 - 1))
    mixed = jax.random.permutation(jax.random.fold_in(own, 3), amount)
    donor, receiver = mixed[0:amount // 2 * 2:2], mixed[1:amount // 2 * 2:2]
    slack = jnp.minimum(lengths[donor] - 1, limit - lengths[receiver]) // 2
    slack = jnp.where((donor == order[0]) | (receiver == order[0]) | (lengths[receiver] == 0), 0, jnp.maximum(slack, 0))
    passed = jax.random.randint(jax.random.fold_in(own, 4), (amount // 2,), 0, 1 << 20) % (slack + 1)
    lengths = lengths.at[donor].add(-passed).at[receiver].add(passed)
    labels = jnp.searchsorted(jnp.cumsum(lengths), jnp.arange(rows * top), side="right").astype(jnp.int32)
    grid = labels.reshape(top, rows).T
    grid = grid[jax.random.permutation(jax.random.fold_in(own, 1), rows)]
    turn = jax.random.randint(jax.random.fold_in(own, 2), (rows, 1), 0, top)
    return jnp.take_along_axis(grid, (jnp.arange(top)[None, :] + turn) % top, axis=1)


def load_shares(number_of, total, limit, skew, full):
    loads = [(1 << 20) // math.isqrt(grade ** skew) + 1 for grade in range(1, number_of + 1)]
    largest = limit if full else min(limit, max(-(-total // number_of), total * loads[0] // sum(loads)))
    least = 1 if total - largest >= number_of - 1 else 0
    holding, spare = [largest] + [least] * (number_of - 1), total - largest - least * (number_of - 1)
    while spare > 0:
        movable = [i for i in range(1, number_of) if holding[i] < largest] or [i for i in range(1, number_of) if holding[i] < limit]
        pool, remaining = sum([loads[i] for i in movable]), spare
        for i in movable:
            extra = min(limit - holding[i], max(1, remaining * loads[i] // pool), spare)
            holding[i] = holding[i] + extra
            spare = spare - extra
    return np.array(holding)


def centred(stream_key, dims, spread, bound, cuts=(), kind=jnp.bfloat16):
    array = spread * jax.random.normal(stream_key, dims, jnp.float32)
    if cuts:
        array = array * steps_of(stream_key, dims, cuts, -0.22, 0.18)
    return jnp.clip(array, -bound, bound).astype(kind)


def setup_inputs(seed: int = 0) -> dict:
    key_of = jax.random.split(jax.random.key(seed), 8)
    activations = centred(key_of[0], (TOKENS, D), 1.0, 6.0, ((0, 128),))
    out_grad = centred(key_of[1], (TOKENS, D), 0.25, 1.5, ((0, 128),))
    expert_ids_keys = jax.random.split(jax.random.fold_in(key_of[2], 1), TOKENS // TOK_DEV)
    expert_ids_turns = jax.random.permutation(jax.random.fold_in(key_of[2], 3), TOKENS // TOK_DEV)
    expert_ids = jax.vmap(lambda own, number: assign_block(jax.random.fold_in(key_of[2], 2), own, number, TOK_DEV, EXPERTS, TOP, CAP, 2))(expert_ids_keys, expert_ids_turns).reshape((TOKENS, TOP))
    gate_probs = jnp.clip(0.049804688 + 0.9501953 * jax.random.uniform(key_of[3], (TOKENS, TOP), jnp.float32) ** steps_of(key_of[3], (TOKENS, TOP), ((0, 128),), -0.2, 0.2), 0.049804688, 1.0).astype(jnp.bfloat16)
    gate_weight = centred(key_of[4], (EXPERTS, D, F), D ** -0.5, 0.09375, ((0, 64), (1, 2)))
    up_weight = centred(key_of[5], (EXPERTS, D, F), D ** -0.5, 0.09375, ((0, 64), (1, 2)))
    down_weight = centred(key_of[6], (EXPERTS, D, F), F ** -0.5, 0.1875, ((0, 64), (1, 2)))
    return dict(activations=activations, out_grad=out_grad, expert_ids=expert_ids, gate_probs=gate_probs, gate_weight=gate_weight, up_weight=up_weight, down_weight=down_weight)


def activate(summed, prob_rows, hidden):
    pre_gate = summed[:, :hidden]
    pre_up = summed[:, hidden:2 * hidden]
    raw_grad = summed[:, 2 * hidden:]
    sigmoid_gate = jax.nn.sigmoid(pre_gate)
    silu_gate = pre_gate * sigmoid_gate
    hidden_rows = (silu_gate * pre_up).astype(jnp.bfloat16)
    scaled_grad = prob_rows.astype(jnp.float32)[:, None] * raw_grad
    slope = sigmoid_gate * (1.0 + pre_gate * (1.0 - sigmoid_gate))
    gate_rows = (scaled_grad * pre_up * slope).astype(jnp.bfloat16)
    up_rows = (scaled_grad * silu_gate).astype(jnp.bfloat16)
    return hidden_rows, gate_rows, up_rows


def reference(activations, out_grad, expert_ids, gate_probs, gate_weight, up_weight, down_weight):
    routes = expert_ids[:, 0].astype(jnp.int32)
    feature_width = activations.shape[1]
    hidden = gate_weight.shape[2]
    expert_total = gate_weight.shape[0]
    blocks = N_DP
    block_width = feature_width // blocks
    row_bound = CAP * N_EXPERT * N_DP
    onehot = (routes[:, None] == jnp.arange(expert_total, dtype=jnp.int32)[None, :]).astype(jnp.int32)
    counts = jnp.sum(onehot, axis=0).astype(jnp.int32)
    offsets = (jnp.cumsum(counts) - counts).astype(jnp.int32)
    sorted_order = jnp.argsort(routes, stable=True).astype(jnp.int32)
    padded_order = jnp.concatenate([sorted_order, jnp.zeros((row_bound,), jnp.int32)])

    def per_expert(expert):
        picked = lax.dynamic_slice_in_dim(padded_order, offsets[expert], row_bound)
        live_rows = jnp.arange(row_bound, dtype=jnp.int32) < counts[expert]
        row_tokens = jnp.where(live_rows[:, None], activations[picked], 0).astype(jnp.bfloat16)
        row_grads = jnp.where(live_rows[:, None], out_grad[picked], 0).astype(jnp.bfloat16)
        prob_rows = jnp.where(live_rows, gate_probs[picked, 0], 0).astype(jnp.bfloat16)
        w_gate = gate_weight[expert].astype(jnp.float32)
        w_up = up_weight[expert].astype(jnp.float32)
        w_down = down_weight[expert].astype(jnp.float32)
        token_blocks = row_tokens.astype(jnp.float32).reshape(row_bound, blocks, block_width)
        grad_blocks = row_grads.astype(jnp.float32).reshape(row_bound, blocks, block_width)

        def block_sum(left, weight):
            parts = jnp.einsum("rkd,kdf->rkf", left, weight.reshape(blocks, block_width, hidden))
            parts = lax.optimization_barrier(parts.astype(jnp.bfloat16))
            return jnp.sum(parts.astype(jnp.float32), axis=1)

        summed = jnp.concatenate([block_sum(token_blocks, w_gate), block_sum(token_blocks, w_up), block_sum(grad_blocks, w_down)], axis=1)
        hidden_rows, gate_rows, up_rows = activate(summed, prob_rows, hidden)
        scaled_hidden = (prob_rows.astype(jnp.float32)[:, None] * hidden_rows.astype(jnp.float32)).astype(jnp.bfloat16)
        gate_f = gate_rows.astype(jnp.float32)
        up_f = up_rows.astype(jnp.float32)
        input_rows = (jnp.einsum("rf,df->rd", gate_f, w_gate) + jnp.einsum("rf,df->rd", up_f, w_up)).astype(jnp.bfloat16)
        tokens_f = row_tokens.astype(jnp.float32)
        grads_f = row_grads.astype(jnp.float32)
        gate_grad = jnp.einsum("rd,rf->df", tokens_f, gate_f).astype(jnp.bfloat16)
        up_grad = jnp.einsum("rd,rf->df", tokens_f, up_f).astype(jnp.bfloat16)
        down_grad = jnp.einsum("rd,rf->df", grads_f, scaled_hidden.astype(jnp.float32)).astype(jnp.bfloat16)
        expert_out = jnp.einsum("rf,df->rd", hidden_rows.astype(jnp.float32), w_down)
        prob_rows_out = jnp.sum(grads_f * expert_out, axis=1).astype(jnp.bfloat16)
        return input_rows, prob_rows_out, gate_grad, up_grad, down_grad

    results = lax.map(per_expert, jnp.arange(expert_total, dtype=jnp.int32))
    positions = jnp.zeros_like(sorted_order).at[sorted_order].set(jnp.arange(sorted_order.shape[0], dtype=jnp.int32))
    slot_index = (positions - offsets[routes]).astype(jnp.int32)
    input_delta = results[0][routes, slot_index]
    prob_delta = results[1][routes, slot_index][:, None]
    return input_delta, prob_delta, results[2], results[3], results[4]
```

```python
import functools

import jax
import jax.numpy as jnp
from jax import lax
from jax.experimental import pallas as pl
from jax.experimental.pallas import tpu as pltpu
from jax.sharding import PartitionSpec as P

MESH = pl.DeviceIdType.MESH
BF = jnp.bfloat16
F32 = jnp.float32
TOK = 128
CAP = 6
SLAB = 4 * CAP
GROUP = 8
ROWS = GROUP * SLAB
WIDE = 1792
HID = 1024
EXTRA = 128
TILE = 256


def rem(a, b):
    return lax.rem(a, jnp.int32(b))


def div(a, b):
    return lax.div(a, jnp.int32(b))


def dot(a, b, dims):
    return lax.dot_general(a, b, ((dims[:1], dims[1:]), ((), ())), preferred_element_type=F32)


def kernel(
    ids_col, ids_row, p_row, p_col, x, g, wg, wu, wd,
    dx, dprob, gg, gu, gd,
    vw, meta, xr, gr, one, onep, onet, sx, sg, x3, g3,
    pgu, pr, qgu, qr, rows_gu, rows_h, b3, r3, out_s, out_r,
    w_sem, m_send, m_recv, x_send, x_recv, y_send, y_recv, d_send, d_recv,
    b_send, b_recv, o_send, o_recv, g_sem,
):
    e = lax.axis_index("expert")
    xl = lax.axis_index("dp")
    core, xh, y, z = rem(e, 2), rem(div(e, 2), 2), rem(div(e, 4), 4), div(e, 16)
    mine = xh * 2 + xl
    own_slab = div(e, 4) * 2 + core

    def mate(i):
        th, tl = rem(xh + i // 2, 2), rem(xl + i % 2, 2)
        return th, tl, th * 2 + tl, (div(e, 4) * 4 + th * 2 + core, tl)

    def plane(q, sign):
        dz = rem(div(q * (q + 1), 2), 4)
        return rem(z + dz if sign > 0 else z + 4 - dz, 4)

    def half(ref, k):
        return ref.at[:, pl.ds(pl.multiple_of(k * WIDE, WIDE), WIDE)]

    def part(ref, m):
        return ref.at[pl.ds(pl.multiple_of(m * TOK, TOK), TOK)]

    for i, w in enumerate((wg, wu, wd)):
        pltpu.make_async_copy(w.at[0], vw.at[i], w_sem.at[i]).start()

    def x_copy(a, src, dst, i):
        _, tl, m, where = mate(i)
        return pltpu.make_async_remote_copy(
            src_ref=half(src, tl), dst_ref=part(dst, mine),
            send_sem=x_send.at[a, i], recv_sem=x_recv.at[a, i],
            device_id=where, device_id_type=MESH,
        )

    def x_own(a, src, dst):
        return pltpu.make_async_copy(half(src, xl), part(dst, mine), x_recv.at[a, 0])

    for i in (2, 1, 3):
        x_copy(0, x, xr, i).start()
    x_own(0, x, xr).start()

    ids = ids_row[...]
    before = lax.broadcasted_iota(jnp.int32, (TOK, TOK), 0) < lax.broadcasted_iota(
        jnp.int32, (TOK, TOK), 1
    )
    same = jnp.where((ids_col[...] == ids) & before, 1.0, 0.0)
    rank = jnp.sum(same, axis=0, keepdims=True)
    side = ((ids >> 1) & 1).astype(F32)
    row = ((ids >> 2) * 2 + (ids & 1)) * SLAB + mine * CAP
    meta[mine, 0:1, :] = side
    meta[mine, 1:2, :] = row.astype(F32) + rank
    meta[mine, 2:3, :] = p_row[...]
    meta[mine, 3:8, :] = jnp.zeros((5, TOK), F32)

    def m_copy(i):
        return pltpu.make_async_remote_copy(
            src_ref=meta.at[mine], dst_ref=meta.at[mine],
            send_sem=m_send.at[i], recv_sem=m_recv.at[i],
            device_id=mate(i)[3], device_id_type=MESH,
        )

    for i in (2, 1, 3):
        m_copy(i).start()
    for i in (2, 1, 3):
        x_copy(1, g, gr, i).start()
    x_own(1, g, gr).start()

    for i in (1, 2, 3):
        m_copy(i).wait_recv()
    my_side = xh.astype(F32)
    for m in range(4):
        want = jnp.where(meta[m, 0:1, :] == my_side, meta[m, 1:2, :], -1.0)
        prob = meta[m, 2:3, :]
        for r in range(4):
            at = lax.broadcasted_iota(jnp.int32, (ROWS, TOK), 0).astype(F32) + float(r * ROWS)
            hit = at == want
            one[r * ROWS : (r + 1) * ROWS, m * TOK : (m + 1) * TOK] = jnp.where(
                hit, 1.0, 0.0
            ).astype(BF)
            onep[r * ROWS : (r + 1) * ROWS, m * TOK : (m + 1) * TOK] = jnp.where(
                hit, prob, 0.0
            ).astype(BF)
        down = jnp.transpose(jnp.broadcast_to(want, (TOK, TOK)))
        for r in range(4 * ROWS // TOK):
            at = lax.broadcasted_iota(jnp.int32, (TOK, TOK), 1).astype(F32) + float(r * TOK)
            onet[m * TOK : (m + 1) * TOK, r * TOK : (r + 1) * TOK] = jnp.where(
                at == down, 1.0, 0.0
            ).astype(BF)

    def group_send(q, sign, src, dst, s_sem, r_sem):
        zt = plane(q, sign)

        def one_send(i, _):
            yt, ct = rem(y + div(i, 2), 4), rem(core + rem(i, 2), 2)
            pltpu.make_async_remote_copy(
                src_ref=src.at[(zt * 4 + yt) * 2 + ct], dst_ref=dst.at[own_slab],
                send_sem=s_sem, recv_sem=r_sem,
                device_id=(((zt * 4 + yt) * 2 + xh) * 2 + ct, xl), device_id_type=MESH,
            ).start()
            return 0

        first = jnp.where(q == 0, 1, 0).astype(jnp.int32) if not isinstance(q, int) else int(q == 0)
        lax.fori_loop(first, GROUP, one_send, 0)

    def group_wait(count, first, src, dst, sem):
        pltpu.make_async_copy(
            src.at[pl.ds(first, count)], dst.at[pl.ds(first, count)], sem
        ).wait()

    def gather_and_send(a, picks, rows, src, dst):
        for q in range(4):
            zt = plane(jnp.int32(q), 1)

            @pl.loop(0, WIDE // TILE)
            def _(n):
                lanes = pl.ds(pl.multiple_of(n * TILE, TILE), TILE)
                got = dot(picks[pl.ds(pl.multiple_of(zt * ROWS, ROWS), ROWS), :], rows[:, lanes], (1, 0))
                src[pl.ds(zt * GROUP, GROUP), :, lanes] = got.astype(BF).reshape(GROUP, SLAB, TILE)

            group_send(q, 1, src, dst, y_send.at[a, q], y_recv.at[a, q])
            if q == 0:
                pltpu.make_async_copy(src.at[own_slab], dst.at[own_slab], y_recv.at[a, 0]).start()

    for i in (1, 2, 3):
        x_copy(0, x, xr, i).wait_recv()
    x_own(0, x, xr).wait()
    gather_and_send(0, one, xr, sx, x3)
    for i in (1, 2, 3):
        x_copy(1, g, gr, i).wait_recv()
    x_own(1, g, gr).wait()
    gather_and_send(1, onep, gr, sg, g3)

    other = (e, 1 - xl)

    def d_copy(a, q):
        src, dst = ((pgu, qgu), (pr, qr))[a]
        at = plane(q, -1)
        return pltpu.make_async_remote_copy(
            src_ref=src.at[at], dst_ref=dst.at[at],
            send_sem=d_send.at[a, q], recv_sem=d_recv.at[a, q],
            device_id=other, device_id_type=MESH,
        )

    for i, w in enumerate((wg, wu, wd)):
        pltpu.make_async_copy(w.at[0], vw.at[i], w_sem.at[i]).wait()

    @pl.loop(0, 4)
    def _(q):
        at = plane(q, -1)
        group_wait(GROUP, at * GROUP, sx, x3, y_recv.at[0, q])

        @pl.loop(0, HID // TILE)
        def _(n):
            lanes = pl.ds(pl.multiple_of(n * TILE, TILE), TILE)
            more = pl.ds(pl.multiple_of(HID + n * TILE, TILE), TILE)
            left = x3[pl.ds(at * GROUP, GROUP)].reshape(ROWS, WIDE)
            pgu[at, :, lanes] = dot(left, vw[0, :, lanes], (1, 0)).astype(BF)
            pgu[at, :, more] = dot(left, vw[1, :, lanes], (1, 0)).astype(BF)

        d_copy(0, q).start()

    @pl.loop(0, 4)
    def _(q):
        at = plane(q, -1)
        group_wait(GROUP, at * GROUP, sg, g3, y_recv.at[1, q])

        @pl.loop(0, HID // TILE)
        def _(n):
            lanes = pl.ds(pl.multiple_of(n * TILE, TILE), TILE)
            left = g3[pl.ds(at * GROUP, GROUP)].reshape(ROWS, WIDE)
            pr[at, :, lanes] = dot(left, vw[2, :, lanes], (1, 0)).astype(BF)

        d_copy(1, q).start()

    for q in range(4):
        at = plane(jnp.int32(q), -1)
        d_copy(0, jnp.int32(q)).wait_recv()
        d_copy(1, jnp.int32(q)).wait_recv()
        here = pl.ds(pl.multiple_of(at * ROWS, ROWS), ROWS)

        def act(n, total):
            lanes = pl.ds(pl.multiple_of(n * TILE, TILE), TILE)
            more = pl.ds(pl.multiple_of(HID + n * TILE, TILE), TILE)
            gate = pgu[at, :, lanes].astype(F32) + qgu[at, :, lanes].astype(F32)
            up = pgu[at, :, more].astype(F32) + qgu[at, :, more].astype(F32)
            d = pr[at, :, lanes].astype(F32) + qr[at, :, lanes].astype(F32)
            s = jax.nn.sigmoid(gate)
            silu = gate * s
            hidden = silu * up
            rows_h[here, lanes] = hidden.astype(BF)
            rows_gu[here, lanes] = (d * up * (s * (1.0 + gate * (1.0 - s)))).astype(BF)
            rows_gu[here, more] = (d * silu).astype(BF)
            return total + jnp.sum(hidden * d, axis=1, keepdims=True)

        total = lax.fori_loop(0, HID // TILE, act, jnp.zeros((ROWS, 1), F32))
        b3[pl.ds(at * GROUP, GROUP), :, WIDE:] = (
            jnp.broadcast_to(total, (ROWS, EXTRA)).astype(BF).reshape(GROUP, SLAB, EXTRA)
        )

        @pl.loop(0, WIDE // TILE)
        def _(n):
            lanes = pl.ds(pl.multiple_of(n * TILE, TILE), TILE)
            back = dot(rows_gu[here, :HID], vw[0, lanes, :], (1, 1)) + dot(
                rows_gu[here, HID:], vw[1, lanes, :], (1, 1)
            )
            b3[pl.ds(at * GROUP, GROUP), :, lanes] = back.astype(BF).reshape(GROUP, SLAB, TILE)

        group_send(q, -1, b3, r3, b_send.at[q], b_recv.at[q])
        if q == 0:
            pltpu.make_async_copy(b3.at[own_slab], r3.at[own_slab], b_recv.at[0]).start()

    def g_copy(i, n):
        rows = pl.ds(pl.multiple_of(n * TILE, TILE), TILE)
        return pltpu.make_async_copy(vw.at[i, rows], (gg, gu, gd)[i].at[0, rows], g_sem.at[i, n])

    @pl.loop(0, WIDE // TILE)
    def _(n):
        lanes = pl.ds(pl.multiple_of(n * TILE, TILE), TILE)
        left = x3[:, :, lanes].reshape(4 * ROWS, TILE)
        vw[0, lanes, :] = dot(left, rows_gu[:, :HID], (0, 0)).astype(BF)
        vw[1, lanes, :] = dot(left, rows_gu[:, HID:], (0, 0)).astype(BF)
        g_copy(0, n).start()
        g_copy(1, n).start()

    for q in range(4):
        group_wait(GROUP, plane(jnp.int32(q), 1) * GROUP, b3, r3, b_recv.at[q])

    def pick(m):
        return dot(
            onet[pl.ds(pl.multiple_of(m * TOK, TOK), TOK), :],
            r3[...].reshape(4 * ROWS, WIDE + EXTRA), (1, 0),
        ).astype(BF)

    def o_copy(i):
        _, _, m, where = mate(i)
        return pltpu.make_async_remote_copy(
            src_ref=out_s.at[m], dst_ref=out_r.at[mine],
            send_sem=o_send.at[i], recv_sem=o_recv.at[i],
            device_id=where, device_id_type=MESH,
        )

    for i in (2, 1, 3):
        m = mate(i)[2]
        out_s[m] = pick(m)
        o_copy(i).start()
    out_r[mine] = pick(mine)

    @pl.loop(0, WIDE // TILE)
    def _(n):
        lanes = pl.ds(pl.multiple_of(n * TILE, TILE), TILE)
        left = g3[:, :, lanes].reshape(4 * ROWS, TILE)
        vw[2, lanes, :] = dot(left, rows_h[...], (0, 0)).astype(BF)
        g_copy(2, n).start()

    for i in (1, 2, 3):
        o_copy(i).wait_recv()
    for k in range(2):
        dx[:, k * WIDE : (k + 1) * WIDE] = (
            out_r[k, :, :WIDE].astype(F32) + out_r[2 + k, :, :WIDE].astype(F32)
        ).astype(BF)
    term = out_r[0, :, WIDE : WIDE + 1].astype(F32) + out_r[2, :, WIDE : WIDE + 1].astype(F32)
    dprob[...] = (term / p_col[...].astype(F32)).astype(BF)

    for i in (1, 2, 3):
        m_copy(i).wait_send()
        x_copy(0, x, xr, i).wait_send()
        x_copy(1, g, gr, i).wait_send()
        o_copy(i).wait_send()
    for q in range(4):
        count = GROUP - (q == 0)
        group_wait(count, 0, sx, x3, y_send.at[0, q])
        group_wait(count, 0, sg, g3, y_send.at[1, q])
        group_wait(count, 0, b3, r3, b_send.at[q])
        d_copy(0, jnp.int32(q)).wait_send()
        d_copy(1, jnp.int32(q)).wait_send()
    for n in range(WIDE // TILE):
        for i in range(3):
            g_copy(i, n).wait()


def on_device(activations, out_grad, expert_ids, gate_probs, gate_weight, up_weight, down_weight):
    vmem = pl.BlockSpec(memory_space=pltpu.VMEM)
    hbm = pl.BlockSpec(memory_space=pl.ANY)
    dma = pltpu.SemaphoreType.DMA
    slabs = (4 * GROUP, SLAB, WIDE)
    grad = jax.ShapeDtypeStruct((1, WIDE, HID), BF)
    return tuple(
        pl.pallas_call(
            kernel,
            out_shape=(
                jax.ShapeDtypeStruct((TOK, 2 * WIDE), BF),
                jax.ShapeDtypeStruct((TOK, 1), BF),
                grad, grad, grad,
            ),
            in_specs=[vmem] * 4 + [hbm] * 5,
            out_specs=(vmem, vmem, hbm, hbm, hbm),
            scratch_shapes=[
                pltpu.VMEM((3, WIDE, HID), BF),
                pltpu.VMEM((4, 8, TOK), F32),
                pltpu.VMEM((4 * TOK, WIDE), BF),
                pltpu.VMEM((4 * TOK, WIDE), BF),
                pltpu.VMEM((4 * ROWS, 4 * TOK), BF),
                pltpu.VMEM((4 * ROWS, 4 * TOK), BF),
                pltpu.VMEM((4 * TOK, 4 * ROWS), BF),
                pltpu.VMEM(slabs, BF), pltpu.VMEM(slabs, BF),
                pltpu.VMEM(slabs, BF), pltpu.VMEM(slabs, BF),
                pltpu.VMEM((4, ROWS, 2 * HID), BF), pltpu.VMEM((4, ROWS, HID), BF),
                pltpu.VMEM((4, ROWS, 2 * HID), BF), pltpu.VMEM((4, ROWS, HID), BF),
                pltpu.VMEM((4 * ROWS, 2 * HID), BF), pltpu.VMEM((4 * ROWS, HID), BF),
                pltpu.VMEM((4 * GROUP, SLAB, WIDE + EXTRA), BF),
                pltpu.VMEM((4 * GROUP, SLAB, WIDE + EXTRA), BF),
                pltpu.VMEM((4, TOK, WIDE + EXTRA), BF),
                pltpu.VMEM((4, TOK, WIDE + EXTRA), BF),
                dma((3,)), dma((4,)), dma((4,)), dma((2, 4)), dma((2, 4)), dma((2, 4)), dma((2, 4)),
                dma((2, 4)), dma((2, 4)), dma((4,)), dma((4,)), dma((4,)), dma((4,)),
                dma((3, WIDE // TILE)),
            ],
            compiler_params=pltpu.CompilerParams(
                has_side_effects=True, vmem_limit_bytes=61 << 20
            ),
            cost_estimate=pl.CostEstimate(
                flops=8 * 2 * 4 * ROWS * WIDE * HID, bytes_accessed=6 * 2 * WIDE * HID, transcendentals=4 * ROWS * HID
            ),
        )(
            expert_ids,
            expert_ids.reshape(1, TOK),
            gate_probs.astype(F32).reshape(1, TOK),
            gate_probs,
            activations, out_grad, gate_weight, up_weight, down_weight,
        )
    )


def solution(mesh):
    rows, weights = P(("expert", "dp"), None), P("expert", "dp", None)
    return jax.shard_map(
        on_device,
        mesh=mesh,
        in_specs=(rows, rows, rows, rows, weights, weights, weights),
        out_specs=(rows, rows, weights, weights, weights),
        check_vma=False,
    )
```

```python
import functools

import jax
import jax.numpy as jnp
from jax import lax
from jax.experimental import pallas as pl
from jax.experimental.pallas import tpu as pltpu
from jax.sharding import PartitionSpec as P

MESH = pl.DeviceIdType.MESH
BF = jnp.bfloat16
F32 = jnp.float32
TOK = 128
CAP = 6
SLAB = 4 * CAP
GROUP = 8
ROWS = GROUP * SLAB
WIDE = 1792
HID = 1024
EXTRA = 128
TILE = 256
CUT = 640


def rem(a, b):
    return lax.rem(a, jnp.int32(b))


def div(a, b):
    return lax.div(a, jnp.int32(b))


def dot(a, b, dims):
    return lax.dot_general(a, b, ((dims[:1], dims[1:]), ((), ())), preferred_element_type=F32)


def kernel(
    ids_row, p_row, x, g, wg, wu, wd,
    dx, dprob, vg, vu, vd,
    meta, xv, gv, px, pg, xr, gr, one, onep, onet, sx, sg, x3, g3,
    pgu, pr, qgu, qr, rows_gu, rows_h, b3, r3, out_s, out_r,
    w_sem, m_send, m_recv, x_send, x_recv, y_send, y_recv, d_send, d_recv,
    b_send, b_recv, o_send, o_recv,
):
    e = lax.axis_index("expert")
    xl = lax.axis_index("dp")
    core, xh, y, z = rem(e, 2), rem(div(e, 2), 2), rem(div(e, 4), 4), div(e, 16)
    mine = xh * 2 + xl
    own_slab = div(e, 4) * 2 + core

    def mate(i):
        th, tl = rem(xh + i // 2, 2), rem(xl + i % 2, 2)
        return th, tl, th * 2 + tl, (div(e, 4) * 4 + th * 2 + core, tl)

    def plane(q, sign):
        dz = rem(div(q * (q + 1), 2), 4)
        return rem(z + dz if sign > 0 else z + 4 - dz, 4)

    def half(ref, k):
        return ref.at[:, pl.ds(pl.multiple_of(k * WIDE, WIDE), WIDE)]

    def part(ref, m):
        return ref.at[pl.ds(pl.multiple_of(m * TOK, TOK), TOK)]

    def x_copy(a, i, src, dst, m, where):
        return pltpu.make_async_remote_copy(
            src_ref=src, dst_ref=part(dst, m),
            send_sem=x_send.at[a, i], recv_sem=x_recv.at[a, i],
            device_id=where, device_id_type=MESH,
        )

    def x_near(a, src, dst):
        return x_copy(a, 1, src, dst, mine, mate(1)[3])

    def x_over(a, src, dst):
        return x_copy(a, 3, half(src, 1 - xl), dst, mine, mate(3)[3])

    def x_pass(a, dst):
        m = mate(1)[2]
        return x_copy(a, 2, part(dst, m), dst, m, mate(3)[3])

    def x_own(a, src, dst):
        return pltpu.make_async_copy(half(src, xl), part(dst, mine), x_recv.at[a, 0])

    barrier = pltpu.get_barrier_semaphore()
    for i in (1, 2, 3):
        pl.semaphore_signal(barrier, inc=1, device_id=mate(i)[3], device_id_type=MESH)

    def greet(i, _):
        zt, yt = rem(z + div(i, GROUP), 4), rem(y + div(rem(i, GROUP), 2), 4)
        ct = rem(core + rem(i, 2), 2)
        pl.semaphore_signal(
            barrier, inc=1, device_id=(((zt * 4 + yt) * 2 + xh) * 2 + ct, xl), device_id_type=MESH
        )
        return 0

    lax.fori_loop(1, 4 * GROUP, greet, 0)

    load_x = pltpu.make_async_copy(x, xv, x_send.at[0, 0])
    load_g = pltpu.make_async_copy(g, gv, x_send.at[1, 0])
    load_x.start()
    load_g.start()
    x_own(0, x, xr).start()
    x_own(1, g, gr).start()
    for i, (w, v) in enumerate(((wg, vg), (wu, vu), (wd, vd))):
        pltpu.make_async_copy(w, v, w_sem.at[i]).start()

    ids = ids_row[...]
    side = ((ids >> 1) & 1).astype(F32)
    my_side = xh.astype(F32)
    stay = jnp.transpose(jnp.broadcast_to(side, (TOK, TOK))) == my_side

    def pack(src, dst):
        @pl.loop(0, WIDE // TOK)
        def _(n):
            far = src[:, pl.ds(pl.multiple_of((1 - xl) * WIDE + n * TOK, TOK), TOK)]
            near = src[:, pl.ds(pl.multiple_of(xl * WIDE + n * TOK, TOK), TOK)]
            dst[:, pl.ds(pl.multiple_of(n * TOK, TOK), TOK)] = jnp.where(
                stay, far.astype(F32), near.astype(F32)
            ).astype(BF)

    load_x.wait()
    pack(xv, px)
    pl.semaphore_wait(barrier, 4 * GROUP + 2)
    x_near(0, px, xr).start()
    x_over(0, x, xr).start()

    before = lax.broadcasted_iota(jnp.int32, (TOK, TOK), 0) < lax.broadcasted_iota(
        jnp.int32, (TOK, TOK), 1
    )
    wide_ids = jnp.broadcast_to(ids, (TOK, TOK)).astype(F32)
    same = jnp.where((jnp.transpose(wide_ids) == wide_ids) & before, 1.0, 0.0)
    rank = jnp.sum(same, axis=0, keepdims=True)
    row = ((ids >> 2) * 2 + (ids & 1)) * SLAB + mine * CAP
    meta[mine, 0:1, :] = side
    meta[mine, 1:2, :] = row.astype(F32) + rank
    meta[mine, 2:3, :] = p_row[...].astype(F32)
    meta[mine, 3:8, :] = jnp.zeros((5, TOK), F32)

    def m_copy(i):
        return pltpu.make_async_remote_copy(
            src_ref=meta.at[mine], dst_ref=meta.at[mine],
            send_sem=m_send.at[i], recv_sem=m_recv.at[i],
            device_id=mate(i)[3], device_id_type=MESH,
        )

    for i in (2, 1, 3):
        m_copy(i).start()
    load_g.wait()
    pack(gv, pg)
    x_near(1, pg, gr).start()

    x_near(0, px, xr).wait_recv()
    x_pass(0, xr).start()
    x_over(1, g, gr).start()

    for i in (1, 2, 3):
        m_copy(i).wait_recv()
    for m in range(4):
        want = jnp.where(meta[m, 0:1, :] == my_side, meta[m, 1:2, :], -1.0)
        prob = meta[m, 2:3, :]
        for r in range(4):
            at = lax.broadcasted_iota(jnp.int32, (ROWS, TOK), 0).astype(F32) + float(r * ROWS)
            hit = at == want
            one[r * ROWS : (r + 1) * ROWS, m * TOK : (m + 1) * TOK] = jnp.where(
                hit, 1.0, 0.0
            ).astype(BF)
            onep[r * ROWS : (r + 1) * ROWS, m * TOK : (m + 1) * TOK] = jnp.where(
                hit, prob, 0.0
            ).astype(BF)
        down = jnp.transpose(jnp.broadcast_to(want, (TOK, TOK)))
        for r in range(4 * ROWS // TOK):
            at = lax.broadcasted_iota(jnp.int32, (TOK, TOK), 1).astype(F32) + float(r * TOK)
            onet[m * TOK : (m + 1) * TOK, r * TOK : (r + 1) * TOK] = jnp.where(
                at == down, 1.0, 0.0
            ).astype(BF)

    def group_send(q, sign, src, dst, s_sem, r_sem, lanes=None):
        zt = plane(q, sign)

        def slab(ref, at):
            return ref.at[at] if lanes is None else ref.at[at, :, lanes]

        def one_send(i, _):
            yt, ct = rem(y + div(i, 2), 4), rem(core + rem(i, 2), 2)
            pltpu.make_async_remote_copy(
                src_ref=slab(src, (zt * 4 + yt) * 2 + ct), dst_ref=slab(dst, own_slab),
                send_sem=s_sem, recv_sem=r_sem,
                device_id=(((zt * 4 + yt) * 2 + xh) * 2 + ct, xl), device_id_type=MESH,
            ).start()
            return 0

        first = jnp.where(q == 0, 1, 0).astype(jnp.int32) if not isinstance(q, int) else int(q == 0)
        lax.fori_loop(first, GROUP, one_send, 0)

    def group_wait(count, first, src, dst, sem, lanes=slice(None)):
        pltpu.make_async_copy(
            src.at[pl.ds(first, count), :, lanes], dst.at[pl.ds(first, count), :, lanes], sem
        ).wait()

    def gather_and_send(a, order, picks, rows, src, dst):
        for q in order:
            zt = plane(jnp.int32(q), 1)

            @pl.loop(0, WIDE // TILE)
            def _(n):
                lanes = pl.ds(pl.multiple_of(n * TILE, TILE), TILE)
                here = pl.ds(pl.multiple_of(zt * ROWS, ROWS), ROWS)
                got = dot(picks[here, :], rows[:, lanes], (1, 0)).astype(BF)
                src[pl.ds(zt * GROUP, GROUP), :, lanes] = got.reshape(GROUP, SLAB, TILE)

            group_send(q, 1, src, dst, y_send.at[a, q], y_recv.at[a, q])
            if q == 0:
                pltpu.make_async_copy(src.at[own_slab], dst.at[own_slab], y_recv.at[a, 0]).start()

    x_near(1, pg, gr).wait_recv()
    x_pass(1, gr).start()
    x_over(0, x, xr).wait_recv()
    x_pass(0, xr).wait_recv()
    x_own(0, x, xr).wait()
    gather_and_send(0, (0, 1, 2, 3), one, xr, sx, x3)

    other = (e, 1 - xl)

    def d_copy(a, q):
        src, dst = ((pgu, qgu), (pr, qr))[a]
        at = plane(q, -1)
        return pltpu.make_async_remote_copy(
            src_ref=src.at[at], dst_ref=dst.at[at],
            send_sem=d_send.at[a, q], recv_sem=d_recv.at[a, q],
            device_id=other, device_id_type=MESH,
        )

    for i, (w, v) in enumerate(((wg, vg), (wu, vu), (wd, vd))):
        pltpu.make_async_copy(w, v, w_sem.at[i]).wait()

    def gate_and_up(q, _):
        at = plane(q, -1)
        group_wait(GROUP, at * GROUP, sx, x3, y_recv.at[0, q])

        @pl.loop(0, HID // TILE)
        def _(n):
            lanes = pl.ds(pl.multiple_of(n * TILE, TILE), TILE)
            more = pl.ds(pl.multiple_of(HID + n * TILE, TILE), TILE)
            left = x3[pl.ds(at * GROUP, GROUP)].reshape(ROWS, WIDE)
            pgu[at, :, lanes] = dot(left, vg[0, :, lanes], (1, 0)).astype(BF)
            pgu[at, :, more] = dot(left, vu[0, :, lanes], (1, 0)).astype(BF)

        d_copy(0, q).start()
        return 0

    lax.fori_loop(0, 1, gate_and_up, 0)
    x_over(1, g, gr).wait_recv()
    x_pass(1, gr).wait_recv()
    x_own(1, g, gr).wait()
    gather_and_send(1, (3, 2, 1, 0), onep, gr, sg, g3)

    lax.fori_loop(1, 4, gate_and_up, 0)

    @pl.loop(0, 4)
    def _(step):
        q = 3 - step
        at = plane(q, -1)
        group_wait(GROUP, at * GROUP, sg, g3, y_recv.at[1, q])

        @pl.loop(0, HID // TILE)
        def _(n):
            lanes = pl.ds(pl.multiple_of(n * TILE, TILE), TILE)
            left = g3[pl.ds(at * GROUP, GROUP)].reshape(ROWS, WIDE)
            pr[at, :, lanes] = dot(left, vd[0, :, lanes], (1, 0)).astype(BF)

        d_copy(1, q).start()

    for q in (3, 2, 1, 0):
        at = plane(jnp.int32(q), -1)
        d_copy(0, jnp.int32(q)).wait_recv()
        d_copy(1, jnp.int32(q)).wait_recv()
        here = pl.ds(pl.multiple_of(at * ROWS, ROWS), ROWS)

        def act(n, total):
            lanes = pl.ds(pl.multiple_of(n * TILE, TILE), TILE)
            more = pl.ds(pl.multiple_of(HID + n * TILE, TILE), TILE)
            gate = pgu[at, :, lanes].astype(F32) + qgu[at, :, lanes].astype(F32)
            up = pgu[at, :, more].astype(F32) + qgu[at, :, more].astype(F32)
            d = pr[at, :, lanes].astype(F32) + qr[at, :, lanes].astype(F32)
            s = jax.nn.sigmoid(gate)
            silu = gate * s
            hidden = silu * up
            rows_h[here, lanes] = hidden.astype(BF)
            rows_gu[here, lanes] = (d * up * (s * (1.0 + gate * (1.0 - s)))).astype(BF)
            rows_gu[here, more] = (d * silu).astype(BF)
            return total + jnp.sum(hidden * d, axis=1, keepdims=True)

        total = lax.fori_loop(0, HID // TILE, act, jnp.zeros((ROWS, 1), F32))
        b3[pl.ds(at * GROUP, GROUP), :, WIDE:] = (
            jnp.broadcast_to(total, (ROWS, EXTRA)).astype(BF).reshape(GROUP, SLAB, EXTRA)
        )

        def back(lanes):
            return dot(rows_gu[here, :HID], vg[0, lanes, :], (1, 1)) + dot(
                rows_gu[here, HID:], vu[0, lanes, :], (1, 1)
            )

        if q:

            @pl.loop(0, WIDE // TILE)
            def _(n):
                lanes = pl.ds(pl.multiple_of(n * TILE, TILE), TILE)
                slabs = back(lanes).astype(BF).reshape(GROUP, SLAB, TILE)
                b3[pl.ds(at * GROUP, GROUP), :, lanes] = slabs

            group_send(q, -1, b3, r3, b_send.at[q], b_recv.at[q])
        else:
            for c in range(3):
                width = min(CUT, WIDE - c * CUT)
                lanes = pl.ds(c * CUT, width)
                slabs = back(lanes).astype(BF).reshape(GROUP, SLAB, width)
                b3[pl.ds(at * GROUP, GROUP), :, lanes] = slabs
                sems, lanes = (b_send.at[4 + c], b_recv.at[4 + c]), pl.ds(c * CUT, CUT)
                group_send(q, -1, b3, r3, *sems, lanes)
                pltpu.make_async_copy(
                    b3.at[own_slab, :, lanes], r3.at[own_slab, :, lanes], sems[1]
                ).start()

    for q in (3, 2, 1):
        group_wait(GROUP, plane(jnp.int32(q), 1) * GROUP, b3, r3, b_recv.at[q])

    def o_copy(i, c):
        _, _, m, where = mate(i)
        lanes = pl.ds(c * CUT, CUT)
        return pltpu.make_async_remote_copy(
            src_ref=out_s.at[m, :, lanes], dst_ref=out_r.at[mine, :, lanes],
            send_sem=o_send.at[i, c], recv_sem=o_recv.at[i, c],
            device_id=where, device_id_type=MESH,
        )

    for c in range(3):
        lanes = pl.ds(c * CUT, CUT)
        group_wait(GROUP, z * GROUP, b3, r3, b_recv.at[4 + c], lanes)
        for i in (2, 1, 3, 0):
            m = mate(i)[2]
            picks = onet[pl.ds(pl.multiple_of(m * TOK, TOK), TOK), :]
            got = dot(picks, r3[:, :, lanes].reshape(4 * ROWS, CUT), (1, 0)).astype(BF)
            if i:
                out_s[m, :, lanes] = got
                o_copy(i, c).start()
            else:
                out_r[mine, :, lanes] = got

    @pl.loop(0, WIDE // TILE)
    def _(n):
        lanes = pl.ds(pl.multiple_of(n * TILE, TILE), TILE)
        left = g3[:, :, lanes].reshape(4 * ROWS, TILE)
        vd[0, lanes, :] = dot(left, rows_h[...], (0, 0)).astype(BF)
        left = x3[:, :, lanes].reshape(4 * ROWS, TILE)
        vg[0, lanes, :] = dot(left, rows_gu[:, :HID], (0, 0)).astype(BF)
        vu[0, lanes, :] = dot(left, rows_gu[:, HID:], (0, 0)).astype(BF)

    for c in range(3):
        for i in (1, 2, 3):
            o_copy(i, c).wait_recv()
    for k in range(2):
        dx[:, k * WIDE : (k + 1) * WIDE] = (
            out_r[k, :, :WIDE].astype(F32) + out_r[2 + k, :, :WIDE].astype(F32)
        ).astype(BF)
    term = jnp.transpose(out_r[0, :, WIDE:].astype(F32) + out_r[2, :, WIDE:].astype(F32))
    dprob[...] = (term[0:1] / p_row[...].astype(F32)).astype(BF)

    for i in (1, 2, 3):
        m_copy(i).wait_send()
        for c in range(3):
            o_copy(i, c).wait_send()
    for c in range(3):
        group_wait(GROUP - 1, 0, b3, r3, b_send.at[4 + c], pl.ds(c * CUT, CUT))
    for a, (src, packed, dst) in enumerate(((x, px, xr), (g, pg, gr))):
        x_near(a, packed, dst).wait_send()
        x_over(a, src, dst).wait_send()
        x_pass(a, dst).wait_send()
    for q in range(4):
        count = GROUP - (q == 0)
        group_wait(count, 0, sx, x3, y_send.at[0, q])
        group_wait(count, 0, sg, g3, y_send.at[1, q])
        if q:
            group_wait(count, 0, b3, r3, b_send.at[q])
        d_copy(0, jnp.int32(q)).wait_send()
        d_copy(1, jnp.int32(q)).wait_send()


def place(*refs):
    count = (len(refs) - 1) // 2
    copies = [
        pltpu.make_async_copy(refs[i], refs[count + i], refs[-1].at[i]) for i in range(count)
    ]
    for copy in copies:
        copy.start()
    for copy in copies:
        copy.wait()


def on_device(activations, out_grad, expert_ids, gate_probs, gate_weight, up_weight, down_weight):
    vmem = pl.BlockSpec(memory_space=pltpu.VMEM)
    hbm = pl.BlockSpec(memory_space=pl.ANY)
    dma = pltpu.SemaphoreType.DMA
    slabs = (4 * GROUP, SLAB, WIDE)
    grad = pltpu.VMEM((1, WIDE, HID), BF)
    dx, dprob, *grads = (
        pl.pallas_call(
            kernel,
            out_shape=(
                pltpu.VMEM((TOK, 2 * WIDE), BF),
                pltpu.VMEM((1, TOK), BF),
                grad, grad, grad,
            ),
            in_specs=[vmem] * 2 + [hbm] * 5,
            out_specs=(vmem,) * 5,
            scratch_shapes=[
                pltpu.VMEM((4, 8, TOK), F32),
                pltpu.VMEM((TOK, 2 * WIDE), BF), pltpu.VMEM((TOK, 2 * WIDE), BF),
                pltpu.VMEM((TOK, WIDE), BF), pltpu.VMEM((TOK, WIDE), BF),
                pltpu.VMEM((4 * TOK, WIDE), BF),
                pltpu.VMEM((4 * TOK, WIDE), BF),
                pltpu.VMEM((4 * ROWS, 4 * TOK), BF),
                pltpu.VMEM((4 * ROWS, 4 * TOK), BF),
                pltpu.VMEM((4 * TOK, 4 * ROWS), BF),
                pltpu.VMEM(slabs, BF), pltpu.VMEM(slabs, BF),
                pltpu.VMEM(slabs, BF), pltpu.VMEM(slabs, BF),
                pltpu.VMEM((4, ROWS, 2 * HID), BF), pltpu.VMEM((4, ROWS, HID), BF),
                pltpu.VMEM((4, ROWS, 2 * HID), BF), pltpu.VMEM((4, ROWS, HID), BF),
                pltpu.VMEM((4 * ROWS, 2 * HID), BF), pltpu.VMEM((4 * ROWS, HID), BF),
                pltpu.VMEM((4 * GROUP, SLAB, WIDE + EXTRA), BF),
                pltpu.VMEM((4 * GROUP, SLAB, WIDE + EXTRA), BF),
                pltpu.VMEM((4, TOK, WIDE + EXTRA), BF),
                pltpu.VMEM((4, TOK, WIDE + EXTRA), BF),
                dma((3,)), dma((4,)), dma((4,)), dma((2, 4)), dma((2, 4)), dma((2, 4)), dma((2, 4)),
                dma((2, 4)), dma((2, 4)), dma((7,)), dma((7,)), dma((4, 3)), dma((4, 3)),
            ],
            compiler_params=pltpu.CompilerParams(
                has_side_effects=True, collective_id=0, vmem_limit_bytes=49 << 20
            ),
            cost_estimate=pl.CostEstimate(
                flops=8 * 2 * 4 * ROWS * WIDE * HID, bytes_accessed=6 * 2 * WIDE * HID, transcendentals=4 * ROWS * HID
            ),
        )(
            expert_ids.reshape(1, TOK),
            gate_probs.reshape(1, TOK),
            activations, out_grad, gate_weight, up_weight, down_weight,
        )
    )
    made = [pltpu.with_memory_space_constraint(a, pltpu.VMEM) for a in (dx, dprob, *grads)]
    dx, dprob, *grads = pl.pallas_call(
        place,
        out_shape=[jax.ShapeDtypeStruct(a.shape, a.dtype) for a in made],
        in_specs=[vmem] * 5,
        out_specs=[hbm] * 5,
        scratch_shapes=[dma((5,))],
        compiler_params=pltpu.CompilerParams(vmem_limit_bytes=1 << 20),
    )(*made)
    return dx, dprob.reshape(TOK, 1), *grads


def solution(mesh):
    rows, weights = P(("expert", "dp"), None), P("expert", "dp", None)
    return jax.shard_map(
        on_device,
        mesh=mesh,
        in_specs=(rows, rows, rows, rows, weights, weights, weights),
        out_specs=(rows, rows, weights, weights, weights),
        check_vma=False,
    )
```

```python
import functools

import jax
import jax.numpy as jnp
from jax import lax
from jax.experimental import pallas as pl
from jax.experimental.pallas import tpu as pltpu
from jax.sharding import PartitionSpec as P

MESH = pl.DeviceIdType.MESH
BF = jnp.bfloat16
F32 = jnp.float32
TOK = 128
CAP = 6
SLAB = 4 * CAP
GROUP = 8
ROWS = GROUP * SLAB
WIDE = 1792
HID = 1024
EXTRA = 128
TILE = 256
PIECES = ((0, 3), (3, 5), (5, 7))


def rem(a, b):
    return lax.rem(a, jnp.int32(b))


def div(a, b):
    return lax.div(a, jnp.int32(b))


def dot(a, b, dims):
    return lax.dot_general(a, b, ((dims[:1], dims[1:]), ((), ())), preferred_element_type=F32)


def kernel(
    ids_row, p_row, x, g, wg, wu, wd,
    dx, dprob, vg, vu, vd,
    meta, xv, gv, px, pg, xr, gr, one, onep, onet, sx, sg, x3, g3,
    pgu, pr, qgu, qr, rows_gu, rows_h, b3, r3, out_s, out_r,
    w_sem, m_send, m_recv, x_send, x_recv, y_send, y_recv, d_send, d_recv,
    b_send, b_recv, o_send, o_recv,
):
    e = lax.axis_index("expert")
    xl = lax.axis_index("dp")
    core, xh, y, z = rem(e, 2), rem(div(e, 2), 2), rem(div(e, 4), 4), div(e, 16)
    mine = xh * 2 + xl
    own_slab = div(e, 4) * 2 + core

    def mate(i):
        th, tl = rem(xh + i // 2, 2), rem(xl + i % 2, 2)
        return th, tl, th * 2 + tl, (div(e, 4) * 4 + th * 2 + core, tl)

    def plane(q, sign):
        dz = rem(div(q * (q + 1), 2), 4)
        return rem(z + dz if sign > 0 else z + 4 - dz, 4)

    def half(ref, k):
        return ref.at[:, pl.ds(pl.multiple_of(k * WIDE, WIDE), WIDE)]

    def part(ref, m):
        return ref.at[pl.ds(pl.multiple_of(m * TOK, TOK), TOK)]

    def x_copy(a, i, src, dst, m, where):
        return pltpu.make_async_remote_copy(
            src_ref=src, dst_ref=part(dst, m),
            send_sem=x_send.at[a, i], recv_sem=x_recv.at[a, i],
            device_id=where, device_id_type=MESH,
        )

    def x_near(a, src, dst):
        return x_copy(a, 1, src, dst, mine, mate(1)[3])

    def x_over(a, src, dst):
        return x_copy(a, 3, half(src, 1 - xl), dst, mine, mate(3)[3])

    def x_pass(a, dst):
        m = mate(1)[2]
        return x_copy(a, 2, part(dst, m), dst, m, mate(3)[3])

    def x_own(a, src, dst):
        return pltpu.make_async_copy(half(src, xl), part(dst, mine), x_recv.at[a, 0])

    barrier = pltpu.get_barrier_semaphore()
    for i in (1, 2, 3):
        pl.semaphore_signal(barrier, inc=1, device_id=mate(i)[3], device_id_type=MESH)

    def greet(i, _):
        zt, yt = rem(z + div(i, GROUP), 4), rem(y + div(rem(i, GROUP), 2), 4)
        ct = rem(core + rem(i, 2), 2)
        pl.semaphore_signal(
            barrier, inc=1, device_id=(((zt * 4 + yt) * 2 + xh) * 2 + ct, xl), device_id_type=MESH
        )
        return 0

    lax.fori_loop(1, 4 * GROUP, greet, 0)

    load_x = pltpu.make_async_copy(x, xv, x_send.at[0, 0])
    load_g = pltpu.make_async_copy(g, gv, x_send.at[1, 0])
    load_x.start()
    load_g.start()
    x_own(0, x, xr).start()
    x_own(1, g, gr).start()
    for i, (w, v) in enumerate(((wg, vg), (wu, vu), (wd, vd))):
        pltpu.make_async_copy(w, v, w_sem.at[i]).start()

    ids = ids_row[...]
    side = ((ids >> 1) & 1).astype(F32)
    my_side = xh.astype(F32)
    stay = jnp.transpose(jnp.broadcast_to(side, (TOK, TOK))) == my_side

    def pack(src, dst):
        @pl.loop(0, WIDE // TOK)
        def _(n):
            far = src[:, pl.ds(pl.multiple_of((1 - xl) * WIDE + n * TOK, TOK), TOK)]
            near = src[:, pl.ds(pl.multiple_of(xl * WIDE + n * TOK, TOK), TOK)]
            dst[:, pl.ds(pl.multiple_of(n * TOK, TOK), TOK)] = jnp.where(
                stay, far.astype(F32), near.astype(F32)
            ).astype(BF)

    load_x.wait()
    pack(xv, px)
    pl.semaphore_wait(barrier, 4 * GROUP + 2)
    x_near(0, px, xr).start()
    x_over(0, x, xr).start()

    before = lax.broadcasted_iota(jnp.int32, (TOK, TOK), 0) < lax.broadcasted_iota(
        jnp.int32, (TOK, TOK), 1
    )
    wide_ids = jnp.broadcast_to(ids, (TOK, TOK)).astype(F32)
    same = jnp.where((jnp.transpose(wide_ids) == wide_ids) & before, 1.0, 0.0)
    rank = jnp.sum(same, axis=0, keepdims=True)
    row = ((ids >> 2) * 2 + (ids & 1)) * SLAB + mine * CAP
    meta[mine, 0:1, :] = side
    meta[mine, 1:2, :] = row.astype(F32) + rank
    meta[mine, 2:3, :] = p_row[...].astype(F32)
    meta[mine, 3:8, :] = jnp.zeros((5, TOK), F32)

    def m_copy(i):
        return pltpu.make_async_remote_copy(
            src_ref=meta.at[mine], dst_ref=meta.at[mine],
            send_sem=m_send.at[i], recv_sem=m_recv.at[i],
            device_id=mate(i)[3], device_id_type=MESH,
        )

    for i in (2, 1, 3):
        m_copy(i).start()
    load_g.wait()
    pack(gv, pg)
    x_near(1, pg, gr).start()

    x_near(0, px, xr).wait_recv()
    x_pass(0, xr).start()
    x_over(1, g, gr).start()

    for i in (1, 2, 3):
        m_copy(i).wait_recv()
    for m in range(4):
        want = jnp.where(meta[m, 0:1, :] == my_side, meta[m, 1:2, :], -1.0)
        prob = meta[m, 2:3, :]
        for r in range(4):
            at = lax.broadcasted_iota(jnp.int32, (ROWS, TOK), 0).astype(F32) + float(r * ROWS)
            hit = at == want
            one[r * ROWS : (r + 1) * ROWS, m * TOK : (m + 1) * TOK] = jnp.where(
                hit, 1.0, 0.0
            ).astype(BF)
            onep[r * ROWS : (r + 1) * ROWS, m * TOK : (m + 1) * TOK] = jnp.where(
                hit, prob, 0.0
            ).astype(BF)
        down = jnp.transpose(jnp.broadcast_to(want, (TOK, TOK)))
        for r in range(4 * ROWS // TOK):
            at = lax.broadcasted_iota(jnp.int32, (TOK, TOK), 1).astype(F32) + float(r * TOK)
            onet[m * TOK : (m + 1) * TOK, r * TOK : (r + 1) * TOK] = jnp.where(
                at == down, 1.0, 0.0
            ).astype(BF)

    def group_send(q, sign, src, dst, s_sem, r_sem, lanes=None):
        zt = plane(q, sign)

        def slab(ref, at):
            return ref.at[at] if lanes is None else ref.at[at, :, lanes]

        def one_send(i, _):
            yt, ct = rem(y + div(i, 2), 4), rem(core + rem(i, 2), 2)
            pltpu.make_async_remote_copy(
                src_ref=slab(src, (zt * 4 + yt) * 2 + ct), dst_ref=slab(dst, own_slab),
                send_sem=s_sem, recv_sem=r_sem,
                device_id=(((zt * 4 + yt) * 2 + xh) * 2 + ct, xl), device_id_type=MESH,
            ).start()
            return 0

        first = jnp.where(q == 0, 1, 0).astype(jnp.int32)
        lax.fori_loop(first, GROUP, one_send, 0)

    def group_wait(count, first, src, dst, sem, lanes=slice(None)):
        pltpu.make_async_copy(
            src.at[pl.ds(first, count), :, lanes], dst.at[pl.ds(first, count), :, lanes], sem
        ).wait()

    def gather_and_send(a, turn, picks, rows, src, dst):
        @pl.loop(0, 4)
        def _(step):
            q = turn(step)
            zt = plane(q, 1)

            @pl.loop(0, WIDE // TILE)
            def _(n):
                lanes = pl.ds(pl.multiple_of(n * TILE, TILE), TILE)
                here = pl.ds(pl.multiple_of(zt * ROWS, ROWS), ROWS)
                got = dot(picks[here, :], rows[:, lanes], (1, 0)).astype(BF)
                src[pl.ds(zt * GROUP, GROUP), :, lanes] = got.reshape(GROUP, SLAB, TILE)

            group_send(q, 1, src, dst, y_send.at[a, q], y_recv.at[a, q])

            @pl.when(q == 0)
            def _():
                pltpu.make_async_copy(src.at[own_slab], dst.at[own_slab], y_recv.at[a, 0]).start()

    x_near(1, pg, gr).wait_recv()
    x_pass(1, gr).start()
    x_over(0, x, xr).wait_recv()
    x_pass(0, xr).wait_recv()
    x_own(0, x, xr).wait()
    gather_and_send(0, lambda step: step, one, xr, sx, x3)

    other = (e, 1 - xl)

    def d_copy(a, q):
        src, dst = ((pgu, qgu), (pr, qr))[a]
        at = plane(q, -1)
        return pltpu.make_async_remote_copy(
            src_ref=src.at[at], dst_ref=dst.at[at],
            send_sem=d_send.at[a, q], recv_sem=d_recv.at[a, q],
            device_id=other, device_id_type=MESH,
        )

    for i, (w, v) in enumerate(((wg, vg), (wu, vu), (wd, vd))):
        pltpu.make_async_copy(w, v, w_sem.at[i]).wait()

    def gate_and_up(q, _):
        at = plane(q, -1)
        group_wait(GROUP, at * GROUP, sx, x3, y_recv.at[0, q])

        @pl.loop(0, HID // TILE)
        def _(n):
            lanes = pl.ds(pl.multiple_of(n * TILE, TILE), TILE)
            more = pl.ds(pl.multiple_of(HID + n * TILE, TILE), TILE)
            left = x3[pl.ds(at * GROUP, GROUP)].reshape(ROWS, WIDE)
            pgu[at, :, lanes] = dot(left, vg[0, :, lanes], (1, 0)).astype(BF)
            pgu[at, :, more] = dot(left, vu[0, :, lanes], (1, 0)).astype(BF)

        d_copy(0, q).start()
        return 0

    lax.fori_loop(0, 1, gate_and_up, 0)
    x_over(1, g, gr).wait_recv()
    x_pass(1, gr).wait_recv()
    x_own(1, g, gr).wait()
    gather_and_send(1, lambda step: 3 - step, onep, gr, sg, g3)

    lax.fori_loop(1, 4, gate_and_up, 0)

    @pl.loop(0, 4)
    def _(step):
        q = 3 - step
        at = plane(q, -1)
        group_wait(GROUP, at * GROUP, sg, g3, y_recv.at[1, q])

        @pl.loop(0, HID // TILE)
        def _(n):
            lanes = pl.ds(pl.multiple_of(n * TILE, TILE), TILE)
            left = g3[pl.ds(at * GROUP, GROUP)].reshape(ROWS, WIDE)
            pr[at, :, lanes] = dot(left, vd[0, :, lanes], (1, 0)).astype(BF)

        d_copy(1, q).start()

    def piece(c):
        first, end = PIECES[c]
        return pl.ds(first * TILE, (end - first) * TILE + (EXTRA if c == 2 else 0))

    @pl.loop(0, 4)
    def _(step):
        q = 3 - step
        at = plane(q, -1)
        d_copy(0, q).wait_recv()
        d_copy(1, q).wait_recv()
        here = pl.ds(pl.multiple_of(at * ROWS, ROWS), ROWS)

        def act(n, total):
            lanes = pl.ds(pl.multiple_of(n * TILE, TILE), TILE)
            more = pl.ds(pl.multiple_of(HID + n * TILE, TILE), TILE)
            gate = pgu[at, :, lanes].astype(F32) + qgu[at, :, lanes].astype(F32)
            up = pgu[at, :, more].astype(F32) + qgu[at, :, more].astype(F32)
            d = pr[at, :, lanes].astype(F32) + qr[at, :, lanes].astype(F32)
            s = jax.nn.sigmoid(gate)
            silu = gate * s
            hidden = silu * up
            rows_h[here, lanes] = hidden.astype(BF)
            rows_gu[here, lanes] = (d * up * (s * (1.0 + gate * (1.0 - s)))).astype(BF)
            rows_gu[here, more] = (d * silu).astype(BF)
            return total + jnp.sum(hidden * d, axis=1, keepdims=True)

        total = lax.fori_loop(0, HID // TILE, act, jnp.zeros((ROWS, 1), F32))
        b3[pl.ds(at * GROUP, GROUP), :, WIDE:] = (
            jnp.broadcast_to(total, (ROWS, EXTRA)).astype(BF).reshape(GROUP, SLAB, EXTRA)
        )

        @pl.loop(0, WIDE // TILE)
        def _(n):
            lanes = pl.ds(pl.multiple_of(n * TILE, TILE), TILE)
            back = dot(rows_gu[here, :HID], vg[0, lanes, :], (1, 1)) + dot(
                rows_gu[here, HID:], vu[0, lanes, :], (1, 1)
            )
            b3[pl.ds(at * GROUP, GROUP), :, lanes] = back.astype(BF).reshape(GROUP, SLAB, TILE)
            for c in range(3):

                @pl.when(n == PIECES[c][1] - 1)
                def _(c=c):
                    sems = b_send.at[q, c], b_recv.at[q, c]
                    group_send(q, -1, b3, r3, *sems, piece(c))

                    @pl.when(q == 0)
                    def _():
                        pltpu.make_async_copy(
                            b3.at[own_slab, :, piece(c)], r3.at[own_slab, :, piece(c)], sems[1]
                        ).start()

    def o_copy(i, c):
        _, _, m, where = mate(i)
        return pltpu.make_async_remote_copy(
            src_ref=out_s.at[m, :, piece(c)], dst_ref=out_r.at[mine, :, piece(c)],
            send_sem=o_send.at[i, c], recv_sem=o_recv.at[i, c],
            device_id=where, device_id_type=MESH,
        )

    def pick(lanes, width):
        got = dot(onet[...], r3[:, :, lanes].reshape(4 * ROWS, width), (1, 0))
        out_s[:, :, lanes] = got.astype(BF).reshape(4, TOK, width)
        out_r[mine, :, lanes] = out_s[mine, :, lanes]

    @pl.loop(0, WIDE // TILE)
    def _(n):
        for c in range(3):

            @pl.when(n == PIECES[c][0])
            def _(c=c):
                for q in (3, 2, 1, 0):
                    at = plane(jnp.int32(q), 1)
                    group_wait(GROUP, at * GROUP, b3, r3, b_recv.at[q, c], piece(c))

        pick(pl.ds(pl.multiple_of(n * TILE, TILE), TILE), TILE)
        for c in range(3):

            @pl.when(n == PIECES[c][1] - 1)
            def _(c=c):
                if c == 2:
                    pick(pl.ds(WIDE, EXTRA), EXTRA)
                for i in (2, 1, 3):
                    o_copy(i, c).start()

    @pl.loop(0, WIDE // TILE)
    def _(n):
        lanes = pl.ds(pl.multiple_of(n * TILE, TILE), TILE)
        left = g3[:, :, lanes].reshape(4 * ROWS, TILE)
        vd[0, lanes, :] = dot(left, rows_h[...], (0, 0)).astype(BF)
        left = x3[:, :, lanes].reshape(4 * ROWS, TILE)
        vg[0, lanes, :] = dot(left, rows_gu[:, :HID], (0, 0)).astype(BF)
        vu[0, lanes, :] = dot(left, rows_gu[:, HID:], (0, 0)).astype(BF)

    for c in range(3):
        for i in (1, 2, 3):
            o_copy(i, c).wait_recv()
    for k in range(2):
        dx[:, k * WIDE : (k + 1) * WIDE] = (
            out_r[k, :, :WIDE].astype(F32) + out_r[2 + k, :, :WIDE].astype(F32)
        ).astype(BF)
    term = jnp.transpose(out_r[0, :, WIDE:].astype(F32) + out_r[2, :, WIDE:].astype(F32))
    dprob[...] = (term[0:1] / p_row[...].astype(F32)).astype(BF)

    for i in (1, 2, 3):
        m_copy(i).wait_send()
        for c in range(3):
            o_copy(i, c).wait_send()
    for a, (src, packed, dst) in enumerate(((x, px, xr), (g, pg, gr))):
        x_near(a, packed, dst).wait_send()
        x_over(a, src, dst).wait_send()
        x_pass(a, dst).wait_send()
    for q in range(4):
        count = GROUP - (q == 0)
        group_wait(count, 0, sx, x3, y_send.at[0, q])
        group_wait(count, 0, sg, g3, y_send.at[1, q])
        for c in range(3):
            group_wait(count, 0, b3, r3, b_send.at[q, c], piece(c))
        d_copy(0, jnp.int32(q)).wait_send()
        d_copy(1, jnp.int32(q)).wait_send()


def place(*refs):
    count = (len(refs) - 1) // 2
    copies = [
        pltpu.make_async_copy(refs[i], refs[count + i], refs[-1].at[i]) for i in range(count)
    ]
    for copy in copies:
        copy.start()
    for copy in copies:
        copy.wait()


def on_device(activations, out_grad, expert_ids, gate_probs, gate_weight, up_weight, down_weight):
    vmem = pl.BlockSpec(memory_space=pltpu.VMEM)
    hbm = pl.BlockSpec(memory_space=pl.ANY)
    dma = pltpu.SemaphoreType.DMA
    slabs = (4 * GROUP, SLAB, WIDE)
    grad = pltpu.VMEM((1, WIDE, HID), BF)
    dx, dprob, *grads = (
        pl.pallas_call(
            kernel,
            out_shape=(
                pltpu.VMEM((TOK, 2 * WIDE), BF),
                pltpu.VMEM((1, TOK), BF),
                grad, grad, grad,
            ),
            in_specs=[vmem] * 2 + [hbm] * 5,
            out_specs=(vmem,) * 5,
            scratch_shapes=[
                pltpu.VMEM((4, 8, TOK), F32),
                pltpu.VMEM((TOK, 2 * WIDE), BF), pltpu.VMEM((TOK, 2 * WIDE), BF),
                pltpu.VMEM((TOK, WIDE), BF), pltpu.VMEM((TOK, WIDE), BF),
                pltpu.VMEM((4 * TOK, WIDE), BF),
                pltpu.VMEM((4 * TOK, WIDE), BF),
                pltpu.VMEM((4 * ROWS, 4 * TOK), BF),
                pltpu.VMEM((4 * ROWS, 4 * TOK), BF),
                pltpu.VMEM((4 * TOK, 4 * ROWS), BF),
                pltpu.VMEM(slabs, BF), pltpu.VMEM(slabs, BF),
                pltpu.VMEM(slabs, BF), pltpu.VMEM(slabs, BF),
                pltpu.VMEM((4, ROWS, 2 * HID), BF), pltpu.VMEM((4, ROWS, HID), BF),
                pltpu.VMEM((4, ROWS, 2 * HID), BF), pltpu.VMEM((4, ROWS, HID), BF),
                pltpu.VMEM((4 * ROWS, 2 * HID), BF), pltpu.VMEM((4 * ROWS, HID), BF),
                pltpu.VMEM((4 * GROUP, SLAB, WIDE + EXTRA), BF),
                pltpu.VMEM((4 * GROUP, SLAB, WIDE + EXTRA), BF),
                pltpu.VMEM((4, TOK, WIDE + EXTRA), BF),
                pltpu.VMEM((4, TOK, WIDE + EXTRA), BF),
                dma((3,)), dma((4,)), dma((4,)), dma((2, 4)), dma((2, 4)), dma((2, 4)), dma((2, 4)),
                dma((2, 4)), dma((2, 4)), dma((4, 3)), dma((4, 3)), dma((4, 3)), dma((4, 3)),
            ],
            compiler_params=pltpu.CompilerParams(
                has_side_effects=True, collective_id=0, vmem_limit_bytes=49 << 20
            ),
            cost_estimate=pl.CostEstimate(
                flops=8 * 2 * 4 * ROWS * WIDE * HID, bytes_accessed=6 * 2 * WIDE * HID, transcendentals=4 * ROWS * HID
            ),
        )(
            expert_ids.reshape(1, TOK),
            gate_probs.reshape(1, TOK),
            activations, out_grad, gate_weight, up_weight, down_weight,
        )
    )
    made = [pltpu.with_memory_space_constraint(a, pltpu.VMEM) for a in (dx, dprob, *grads)]
    dx, dprob, *grads = pl.pallas_call(
        place,
        out_shape=[jax.ShapeDtypeStruct(a.shape, a.dtype) for a in made],
        in_specs=[vmem] * 5,
        out_specs=[hbm] * 5,
        scratch_shapes=[dma((5,))],
        compiler_params=pltpu.CompilerParams(vmem_limit_bytes=1 << 20),
    )(*made)
    return dx, dprob.reshape(TOK, 1), *grads


def solution(mesh):
    rows, weights = P(("expert", "dp"), None), P("expert", "dp", None)
    return jax.shard_map(
        on_device,
        mesh=mesh,
        in_specs=(rows, rows, rows, rows, weights, weights, weights),
        out_specs=(rows, rows, weights, weights, weights),
        check_vma=False,
    )
```

```python
import functools

import jax
import jax.numpy as jnp
from jax import lax
from jax.experimental import pallas as pl
from jax.experimental.pallas import tpu as pltpu
from jax.sharding import PartitionSpec as P

MESH = pl.DeviceIdType.MESH
BF = jnp.bfloat16
F32 = jnp.float32
TOK = 128
CAP = 6
SLAB = 4 * CAP
GROUP = 8
ROWS = GROUP * SLAB
WIDE = 1792
HID = 1024
EXTRA = 128
TILE = 256
PIECES = ((0, 3), (3, 5), (5, 7))


def rem(a, b):
    return lax.rem(a, jnp.int32(b))


def div(a, b):
    return lax.div(a, jnp.int32(b))


def dot(a, b, dims):
    return lax.dot_general(a, b, ((dims[:1], dims[1:]), ((), ())), preferred_element_type=F32)


def kernel(
    ids_row, p_row, x, g, wg, wu, wd,
    dx, dprob, vg, vu, vd,
    meta, xv, gv, px, pg, xr, gr, one, onep, onet, sx, sg, x3, g3,
    pgu, pr, qgu, qr, rows_gu, rows_h, b3, r3, out_s, out_r,
    w_sem, m_send, m_recv, x_send, x_recv, y_send, y_recv, d_send, d_recv,
    b_send, b_recv, o_send, o_recv,
):
    e = lax.axis_index("expert")
    xl = lax.axis_index("dp")
    core, xh, y, z = rem(e, 2), rem(div(e, 2), 2), rem(div(e, 4), 4), div(e, 16)
    mine = xh * 2 + xl

    def mate(i):
        th, tl = rem(xh + i // 2, 2), rem(xl + i % 2, 2)
        return th, tl, th * 2 + tl, (div(e, 4) * 4 + th * 2 + core, tl)

    def place_of(q, i, sign):
        dz = div(i, 2)
        dy = rem(dz + q, 4)
        zt = rem(z + dz if sign > 0 else z + 4 - dz, 4)
        yt = rem(y + dy if sign > 0 else y + 4 - dy, 4)
        ct = rem(core + rem(i, 2), 2)
        return (((zt * 4 + yt) * 2 + xh) * 2 + ct, xl)

    def half(ref, k):
        return ref.at[:, pl.ds(pl.multiple_of(k * WIDE, WIDE), WIDE)]

    def part(ref, m):
        return ref.at[pl.ds(pl.multiple_of(m * TOK, TOK), TOK)]

    def x_copy(a, i, src, dst, m, where):
        return pltpu.make_async_remote_copy(
            src_ref=src, dst_ref=part(dst, m),
            send_sem=x_send.at[a, i], recv_sem=x_recv.at[a, i],
            device_id=where, device_id_type=MESH,
        )

    def x_near(a, src, dst):
        return x_copy(a, 1, src, dst, mine, mate(1)[3])

    def x_over(a, src, dst):
        return x_copy(a, 3, half(src, 1 - xl), dst, mine, mate(3)[3])

    def x_pass(a, dst):
        m = mate(1)[2]
        return x_copy(a, 2, part(dst, m), dst, m, mate(3)[3])

    def x_own(a, src, dst):
        return pltpu.make_async_copy(half(src, xl), part(dst, mine), x_recv.at[a, 0])

    barrier = pltpu.get_barrier_semaphore()
    for i in (1, 2, 3):
        pl.semaphore_signal(barrier, inc=1, device_id=mate(i)[3], device_id_type=MESH)

    def greet(i, _):
        zt, yt = rem(z + div(i, GROUP), 4), rem(y + div(rem(i, GROUP), 2), 4)
        ct = rem(core + rem(i, 2), 2)
        pl.semaphore_signal(
            barrier, inc=1, device_id=(((zt * 4 + yt) * 2 + xh) * 2 + ct, xl), device_id_type=MESH
        )
        return 0

    lax.fori_loop(1, 4 * GROUP, greet, 0)

    load_x = pltpu.make_async_copy(x, xv, x_send.at[0, 0])
    load_g = pltpu.make_async_copy(g, gv, x_send.at[1, 0])
    load_x.start()
    load_g.start()
    x_own(0, x, xr).start()
    x_own(1, g, gr).start()
    for i, (w, v) in enumerate(((wg, vg), (wu, vu), (wd, vd))):
        pltpu.make_async_copy(w, v, w_sem.at[i]).start()

    ids = ids_row[...]
    side = ((ids >> 1) & 1).astype(F32)
    my_side = xh.astype(F32)
    stay = jnp.transpose(jnp.broadcast_to(side, (TOK, TOK))) == my_side

    def pack(src, dst):
        @pl.loop(0, WIDE // TOK)
        def _(n):
            far = src[:, pl.ds(pl.multiple_of((1 - xl) * WIDE + n * TOK, TOK), TOK)]
            near = src[:, pl.ds(pl.multiple_of(xl * WIDE + n * TOK, TOK), TOK)]
            dst[:, pl.ds(pl.multiple_of(n * TOK, TOK), TOK)] = jnp.where(
                stay, far.astype(F32), near.astype(F32)
            ).astype(BF)

    load_x.wait()
    pack(xv, px)
    pl.semaphore_wait(barrier, 4 * GROUP + 2)
    x_near(0, px, xr).start()
    x_over(0, x, xr).start()

    before = lax.broadcasted_iota(jnp.int32, (TOK, TOK), 0) < lax.broadcasted_iota(
        jnp.int32, (TOK, TOK), 1
    )
    wide_ids = jnp.broadcast_to(ids, (TOK, TOK)).astype(F32)
    same = jnp.where((jnp.transpose(wide_ids) == wide_ids) & before, 1.0, 0.0)
    rank = jnp.sum(same, axis=0, keepdims=True)
    dz = ((ids >> 4) + 4 - z) & 3
    dy = (((ids >> 2) & 3) + 4 - y) & 3
    slab = ((dy + 4 - dz) & 3) * GROUP + dz * 2 + (((ids & 1) + core) & 1)
    row = slab * SLAB + mine * CAP
    meta[mine, 0:1, :] = side
    meta[mine, 1:2, :] = row.astype(F32) + rank
    meta[mine, 2:3, :] = p_row[...].astype(F32)
    meta[mine, 3:8, :] = jnp.zeros((5, TOK), F32)

    def m_copy(i):
        return pltpu.make_async_remote_copy(
            src_ref=meta.at[mine], dst_ref=meta.at[mine],
            send_sem=m_send.at[i], recv_sem=m_recv.at[i],
            device_id=mate(i)[3], device_id_type=MESH,
        )

    for i in (2, 1, 3):
        m_copy(i).start()
    load_g.wait()
    pack(gv, pg)
    x_near(1, pg, gr).start()

    x_near(0, px, xr).wait_recv()
    x_pass(0, xr).start()
    x_over(1, g, gr).start()

    for i in (1, 2, 3):
        m_copy(i).wait_recv()
    for m in range(4):
        want = jnp.where(meta[m, 0:1, :] == my_side, meta[m, 1:2, :], -1.0)
        prob = meta[m, 2:3, :]
        for r in range(4):
            at = lax.broadcasted_iota(jnp.int32, (ROWS, TOK), 0).astype(F32) + float(r * ROWS)
            hit = at == want
            one[r * ROWS : (r + 1) * ROWS, m * TOK : (m + 1) * TOK] = jnp.where(
                hit, 1.0, 0.0
            ).astype(BF)
            onep[r * ROWS : (r + 1) * ROWS, m * TOK : (m + 1) * TOK] = jnp.where(
                hit, prob, 0.0
            ).astype(BF)
        down = jnp.transpose(jnp.broadcast_to(want, (TOK, TOK)))
        for r in range(4 * ROWS // TOK):
            at = lax.broadcasted_iota(jnp.int32, (TOK, TOK), 1).astype(F32) + float(r * TOK)
            onet[m * TOK : (m + 1) * TOK, r * TOK : (r + 1) * TOK] = jnp.where(
                at == down, 1.0, 0.0
            ).astype(BF)

    def group_send(q, sign, src, dst, s_sem, r_sem, lanes=slice(None)):
        def one_send(i, _):
            at = q * GROUP + i
            pltpu.make_async_remote_copy(
                src_ref=src.at[at, :, lanes], dst_ref=dst.at[at, :, lanes],
                send_sem=s_sem, recv_sem=r_sem,
                device_id=place_of(q, i, sign), device_id_type=MESH,
            ).start()
            return 0

        first = jnp.where(q == 0, 1, 0).astype(jnp.int32)
        lax.fori_loop(first, GROUP, one_send, 0)

    def group_wait(count, first, src, dst, sem, lanes=slice(None)):
        pltpu.make_async_copy(
            src.at[pl.ds(first, count), :, lanes], dst.at[pl.ds(first, count), :, lanes], sem
        ).wait()

    def gather_and_send(a, turn, picks, rows, src, dst):
        @pl.loop(0, 4)
        def _(step):
            q = turn(step)

            @pl.loop(0, WIDE // TILE)
            def _(n):
                lanes = pl.ds(pl.multiple_of(n * TILE, TILE), TILE)
                here = pl.ds(pl.multiple_of(q * ROWS, ROWS), ROWS)
                got = dot(picks[here, :], rows[:, lanes], (1, 0)).astype(BF)
                src[pl.ds(q * GROUP, GROUP), :, lanes] = got.reshape(GROUP, SLAB, TILE)

            group_send(q, 1, src, dst, y_send.at[a, q], y_recv.at[a, q])

            @pl.when(q == 0)
            def _():
                pltpu.make_async_copy(src.at[0], dst.at[0], y_recv.at[a, 0]).start()

    x_near(1, pg, gr).wait_recv()
    x_pass(1, gr).start()
    x_over(0, x, xr).wait_recv()
    x_pass(0, xr).wait_recv()
    x_own(0, x, xr).wait()
    gather_and_send(0, lambda step: step, one, xr, sx, x3)

    other = (e, 1 - xl)

    def d_copy(a, q):
        src, dst = ((pgu, qgu), (pr, qr))[a]
        at = q
        return pltpu.make_async_remote_copy(
            src_ref=src.at[at], dst_ref=dst.at[at],
            send_sem=d_send.at[a, q], recv_sem=d_recv.at[a, q],
            device_id=other, device_id_type=MESH,
        )

    for i, (w, v) in enumerate(((wg, vg), (wu, vu), (wd, vd))):
        pltpu.make_async_copy(w, v, w_sem.at[i]).wait()

    def gate_and_up(q, _):
        at = q
        group_wait(GROUP, at * GROUP, sx, x3, y_recv.at[0, q])

        @pl.loop(0, HID // TILE)
        def _(n):
            lanes = pl.ds(pl.multiple_of(n * TILE, TILE), TILE)
            more = pl.ds(pl.multiple_of(HID + n * TILE, TILE), TILE)
            left = x3[pl.ds(at * GROUP, GROUP)].reshape(ROWS, WIDE)
            pgu[at, :, lanes] = dot(left, vg[0, :, lanes], (1, 0)).astype(BF)
            pgu[at, :, more] = dot(left, vu[0, :, lanes], (1, 0)).astype(BF)

        d_copy(0, q).start()
        return 0

    lax.fori_loop(0, 1, gate_and_up, 0)
    x_over(1, g, gr).wait_recv()
    x_pass(1, gr).wait_recv()
    x_own(1, g, gr).wait()
    gather_and_send(1, lambda step: step, onep, gr, sg, g3)

    lax.fori_loop(1, 4, gate_and_up, 0)

    @pl.loop(0, 4)
    def _(step):
        q = step
        at = q
        group_wait(GROUP, at * GROUP, sg, g3, y_recv.at[1, q])

        @pl.loop(0, HID // TILE)
        def _(n):
            lanes = pl.ds(pl.multiple_of(n * TILE, TILE), TILE)
            left = g3[pl.ds(at * GROUP, GROUP)].reshape(ROWS, WIDE)
            pr[at, :, lanes] = dot(left, vd[0, :, lanes], (1, 0)).astype(BF)

        d_copy(1, q).start()

    def piece(c):
        first, end = PIECES[c]
        return pl.ds(first * TILE, (end - first) * TILE + (EXTRA if c == 2 else 0))

    @pl.loop(0, 4)
    def _(step):
        q = step
        at = q
        d_copy(0, q).wait_recv()
        d_copy(1, q).wait_recv()
        here = pl.ds(pl.multiple_of(at * ROWS, ROWS), ROWS)

        def act(n, total):
            lanes = pl.ds(pl.multiple_of(n * TILE, TILE), TILE)
            more = pl.ds(pl.multiple_of(HID + n * TILE, TILE), TILE)
            gate = pgu[at, :, lanes].astype(F32) + qgu[at, :, lanes].astype(F32)
            up = pgu[at, :, more].astype(F32) + qgu[at, :, more].astype(F32)
            d = pr[at, :, lanes].astype(F32) + qr[at, :, lanes].astype(F32)
            s = jax.nn.sigmoid(gate)
            silu = gate * s
            hidden = silu * up
            rows_h[here, lanes] = hidden.astype(BF)
            rows_gu[here, lanes] = (d * up * (s * (1.0 + gate * (1.0 - s)))).astype(BF)
            rows_gu[here, more] = (d * silu).astype(BF)
            return total + jnp.sum(hidden * d, axis=1, keepdims=True)

        total = lax.fori_loop(0, HID // TILE, act, jnp.zeros((ROWS, 1), F32))
        b3[pl.ds(at * GROUP, GROUP), :, WIDE:] = (
            jnp.broadcast_to(total, (ROWS, EXTRA)).astype(BF).reshape(GROUP, SLAB, EXTRA)
        )

        @pl.loop(0, WIDE // TILE)
        def _(n):
            lanes = pl.ds(pl.multiple_of(n * TILE, TILE), TILE)
            back = dot(rows_gu[here, :HID], vg[0, lanes, :], (1, 1)) + dot(
                rows_gu[here, HID:], vu[0, lanes, :], (1, 1)
            )
            b3[pl.ds(at * GROUP, GROUP), :, lanes] = back.astype(BF).reshape(GROUP, SLAB, TILE)
            for c in range(3):

                @pl.when(n == PIECES[c][1] - 1)
                def _(c=c):
                    sems = b_send.at[q, c], b_recv.at[q, c]
                    group_send(q, -1, b3, r3, *sems, piece(c))

                    @pl.when(q == 0)
                    def _():
                        pltpu.make_async_copy(
                            b3.at[0, :, piece(c)], r3.at[0, :, piece(c)], sems[1]
                        ).start()

    def o_copy(i, c):
        _, _, m, where = mate(i)
        return pltpu.make_async_remote_copy(
            src_ref=out_s.at[m, :, piece(c)], dst_ref=out_r.at[mine, :, piece(c)],
            send_sem=o_send.at[i, c], recv_sem=o_recv.at[i, c],
            device_id=where, device_id_type=MESH,
        )

    def pick(lanes, width):
        got = dot(onet[...], r3[:, :, lanes].reshape(4 * ROWS, width), (1, 0))
        out_s[:, :, lanes] = got.astype(BF).reshape(4, TOK, width)
        out_r[mine, :, lanes] = out_s[mine, :, lanes]

    @pl.loop(0, WIDE // TILE)
    def _(n):
        for c in range(3):

            @pl.when(n == PIECES[c][0])
            def _(c=c):
                for q in (3, 2, 1, 0):
                    group_wait(GROUP, q * GROUP, b3, r3, b_recv.at[q, c], piece(c))

        pick(pl.ds(pl.multiple_of(n * TILE, TILE), TILE), TILE)
        for c in range(3):

            @pl.when(n == PIECES[c][1] - 1)
            def _(c=c):
                if c == 2:
                    pick(pl.ds(WIDE, EXTRA), EXTRA)
                for i in (2, 1, 3):
                    o_copy(i, c).start()

    @pl.loop(0, WIDE // TILE)
    def _(n):
        lanes = pl.ds(pl.multiple_of(n * TILE, TILE), TILE)
        left = g3[:, :, lanes].reshape(4 * ROWS, TILE)
        vd[0, lanes, :] = dot(left, rows_h[...], (0, 0)).astype(BF)
        left = x3[:, :, lanes].reshape(4 * ROWS, TILE)
        vg[0, lanes, :] = dot(left, rows_gu[:, :HID], (0, 0)).astype(BF)
        vu[0, lanes, :] = dot(left, rows_gu[:, HID:], (0, 0)).astype(BF)

    for c in range(3):
        for i in (1, 2, 3):
            o_copy(i, c).wait_recv()
    for k in range(2):
        dx[:, k * WIDE : (k + 1) * WIDE] = (
            out_r[k, :, :WIDE].astype(F32) + out_r[2 + k, :, :WIDE].astype(F32)
        ).astype(BF)
    term = jnp.transpose(out_r[0, :, WIDE:].astype(F32) + out_r[2, :, WIDE:].astype(F32))
    dprob[...] = (term[0:1] / p_row[...].astype(F32)).astype(BF)

    for i in (1, 2, 3):
        m_copy(i).wait_send()
        for c in range(3):
            o_copy(i, c).wait_send()
    for a, (src, packed, dst) in enumerate(((x, px, xr), (g, pg, gr))):
        x_near(a, packed, dst).wait_send()
        x_over(a, src, dst).wait_send()
        x_pass(a, dst).wait_send()
    for q in range(4):
        count = GROUP - (q == 0)
        group_wait(count, 0, sx, x3, y_send.at[0, q])
        group_wait(count, 0, sg, g3, y_send.at[1, q])
        for c in range(3):
            group_wait(count, 0, b3, r3, b_send.at[q, c], piece(c))
        d_copy(0, jnp.int32(q)).wait_send()
        d_copy(1, jnp.int32(q)).wait_send()


def place(*refs):
    count = (len(refs) - 1) // 2
    copies = [
        pltpu.make_async_copy(refs[i], refs[count + i], refs[-1].at[i]) for i in range(count)
    ]
    for copy in copies:
        copy.start()
    for copy in copies:
        copy.wait()


def on_device(activations, out_grad, expert_ids, gate_probs, gate_weight, up_weight, down_weight):
    vmem = pl.BlockSpec(memory_space=pltpu.VMEM)
    hbm = pl.BlockSpec(memory_space=pl.ANY)
    dma = pltpu.SemaphoreType.DMA
    slabs = (4 * GROUP, SLAB, WIDE)
    grad = pltpu.VMEM((1, WIDE, HID), BF)
    dx, dprob, *grads = (
        pl.pallas_call(
            kernel,
            out_shape=(
                pltpu.VMEM((TOK, 2 * WIDE), BF),
                pltpu.VMEM((1, TOK), BF),
                grad, grad, grad,
            ),
            in_specs=[vmem] * 2 + [hbm] * 5,
            out_specs=(vmem,) * 5,
            scratch_shapes=[
                pltpu.VMEM((4, 8, TOK), F32),
                pltpu.VMEM((TOK, 2 * WIDE), BF), pltpu.VMEM((TOK, 2 * WIDE), BF),
                pltpu.VMEM((TOK, WIDE), BF), pltpu.VMEM((TOK, WIDE), BF),
                pltpu.VMEM((4 * TOK, WIDE), BF),
                pltpu.VMEM((4 * TOK, WIDE), BF),
                pltpu.VMEM((4 * ROWS, 4 * TOK), BF),
                pltpu.VMEM((4 * ROWS, 4 * TOK), BF),
                pltpu.VMEM((4 * TOK, 4 * ROWS), BF),
                pltpu.VMEM(slabs, BF), pltpu.VMEM(slabs, BF),
                pltpu.VMEM(slabs, BF), pltpu.VMEM(slabs, BF),
                pltpu.VMEM((4, ROWS, 2 * HID), BF), pltpu.VMEM((4, ROWS, HID), BF),
                pltpu.VMEM((4, ROWS, 2 * HID), BF), pltpu.VMEM((4, ROWS, HID), BF),
                pltpu.VMEM((4 * ROWS, 2 * HID), BF), pltpu.VMEM((4 * ROWS, HID), BF),
                pltpu.VMEM((4 * GROUP, SLAB, WIDE + EXTRA), BF),
                pltpu.VMEM((4 * GROUP, SLAB, WIDE + EXTRA), BF),
                pltpu.VMEM((4, TOK, WIDE + EXTRA), BF),
                pltpu.VMEM((4, TOK, WIDE + EXTRA), BF),
                dma((3,)), dma((4,)), dma((4,)), dma((2, 4)), dma((2, 4)), dma((2, 4)), dma((2, 4)),
                dma((2, 4)), dma((2, 4)), dma((4, 3)), dma((4, 3)), dma((4, 3)), dma((4, 3)),
            ],
            compiler_params=pltpu.CompilerParams(
                has_side_effects=True, collective_id=0, vmem_limit_bytes=49 << 20
            ),
            cost_estimate=pl.CostEstimate(
                flops=8 * 2 * 4 * ROWS * WIDE * HID, bytes_accessed=6 * 2 * WIDE * HID, transcendentals=4 * ROWS * HID
            ),
        )(
            expert_ids.reshape(1, TOK),
            gate_probs.reshape(1, TOK),
            activations, out_grad, gate_weight, up_weight, down_weight,
        )
    )
    made = [pltpu.with_memory_space_constraint(a, pltpu.VMEM) for a in (dx, dprob, *grads)]
    dx, dprob, *grads = pl.pallas_call(
        place,
        out_shape=[jax.ShapeDtypeStruct(a.shape, a.dtype) for a in made],
        in_specs=[vmem] * 5,
        out_specs=[hbm] * 5,
        scratch_shapes=[dma((5,))],
        compiler_params=pltpu.CompilerParams(vmem_limit_bytes=1 << 20),
    )(*made)
    return dx, dprob.reshape(TOK, 1), *grads


def solution(mesh):
    rows, weights = P(("expert", "dp"), None), P("expert", "dp", None)
    return jax.shard_map(
        on_device,
        mesh=mesh,
        in_specs=(rows, rows, rows, rows, weights, weights, weights),
        out_specs=(rows, rows, weights, weights, weights),
        check_vma=False,
    )
```

```python
import functools

import jax
import jax.numpy as jnp
from jax import lax
from jax.experimental import pallas as pl
from jax.experimental.pallas import tpu as pltpu
from jax.sharding import PartitionSpec as P

MESH = pl.DeviceIdType.MESH
BF = jnp.bfloat16
F32 = jnp.float32
TOK = 128
CAP = 6
SLAB = 4 * CAP
GROUP = 8
ROWS = GROUP * SLAB
WIDE = 1792
HID = 1024
EXTRA = 128
TILE = 256
PIECES = ((0, 2), (2, 4), (4, 6), (6, 7))


def rem(a, b):
    return lax.rem(a, jnp.int32(b))


def div(a, b):
    return lax.div(a, jnp.int32(b))


def dot(a, b, dims):
    return lax.dot_general(a, b, ((dims[:1], dims[1:]), ((), ())), preferred_element_type=F32)


def kernel(
    ids_row, p_row, x, g, wg, wu, wd,
    dx, dprob, vg, vu, vd,
    meta, xv, gv, px, pg, xr, gr, one, onep, onet, sx, sg, x3, g3,
    pgu, pr, qgu, qr, rows_gu, rows_h, b3, r3, out_s, out_r,
    w_sem, m_send, m_recv, x_send, x_recv, y_send, y_recv, d_send, d_recv,
    b_send, b_recv, o_send, o_recv,
):
    e = lax.axis_index("expert")
    xl = lax.axis_index("dp")
    core, xh, y, z = rem(e, 2), rem(div(e, 2), 2), rem(div(e, 4), 4), div(e, 16)
    mine = xh * 2 + xl

    def mate(i):
        th, tl = rem(xh + i // 2, 2), rem(xl + i % 2, 2)
        return th, tl, th * 2 + tl, (div(e, 4) * 4 + th * 2 + core, tl)

    def place_of(q, i, sign):
        dz = div(i, 2)
        dy = rem(dz + q, 4)
        zt = rem(z + dz if sign > 0 else z + 4 - dz, 4)
        yt = rem(y + dy if sign > 0 else y + 4 - dy, 4)
        ct = rem(core + rem(i, 2), 2)
        return (((zt * 4 + yt) * 2 + xh) * 2 + ct, xl)

    def half(ref, k):
        return ref.at[:, pl.ds(pl.multiple_of(k * WIDE, WIDE), WIDE)]

    def part(ref, m):
        return ref.at[pl.ds(pl.multiple_of(m * TOK, TOK), TOK)]

    def x_copy(a, i, src, dst, m, where):
        return pltpu.make_async_remote_copy(
            src_ref=src, dst_ref=part(dst, m),
            send_sem=x_send.at[a, i], recv_sem=x_recv.at[a, i],
            device_id=where, device_id_type=MESH,
        )

    def x_near(a, src, dst):
        return x_copy(a, 1, src, dst, mine, mate(1)[3])

    def x_over(a, src, dst):
        return x_copy(a, 3, half(src, 1 - xl), dst, mine, mate(3)[3])

    def x_pass(a, dst):
        m = mate(1)[2]
        return x_copy(a, 2, part(dst, m), dst, m, mate(3)[3])

    def x_own(a, src, dst):
        return pltpu.make_async_copy(half(src, xl), part(dst, mine), x_recv.at[a, 0])

    barrier = pltpu.get_barrier_semaphore()
    for i in (1, 2, 3):
        pl.semaphore_signal(barrier, inc=1, device_id=mate(i)[3], device_id_type=MESH)

    def greet(i, _):
        zt, yt = rem(z + div(i, GROUP), 4), rem(y + div(rem(i, GROUP), 2), 4)
        ct = rem(core + rem(i, 2), 2)
        pl.semaphore_signal(
            barrier, inc=1, device_id=(((zt * 4 + yt) * 2 + xh) * 2 + ct, xl), device_id_type=MESH
        )
        return 0

    lax.fori_loop(1, 4 * GROUP, greet, 0)

    load_x = pltpu.make_async_copy(x, xv, x_send.at[0, 0])
    load_g = pltpu.make_async_copy(g, gv, x_send.at[1, 0])
    load_x.start()
    load_g.start()
    x_own(0, x, xr).start()
    x_own(1, g, gr).start()
    for i, (w, v) in enumerate(((wg, vg), (wu, vu), (wd, vd))):
        pltpu.make_async_copy(w, v, w_sem.at[i]).start()

    ids = ids_row[...]
    side = ((ids >> 1) & 1).astype(F32)
    my_side = xh.astype(F32)
    stay = jnp.transpose(jnp.broadcast_to(side, (TOK, TOK))) == my_side

    def pack(src, dst):
        @pl.loop(0, WIDE // TOK)
        def _(n):
            far = src[:, pl.ds(pl.multiple_of((1 - xl) * WIDE + n * TOK, TOK), TOK)]
            near = src[:, pl.ds(pl.multiple_of(xl * WIDE + n * TOK, TOK), TOK)]
            dst[:, pl.ds(pl.multiple_of(n * TOK, TOK), TOK)] = jnp.where(
                stay, far.astype(F32), near.astype(F32)
            ).astype(BF)

    load_x.wait()
    pack(xv, px)
    pl.semaphore_wait(barrier, 4 * GROUP + 2)
    x_near(0, px, xr).start()
    x_over(0, x, xr).start()

    before = lax.broadcasted_iota(jnp.int32, (TOK, TOK), 0) < lax.broadcasted_iota(
        jnp.int32, (TOK, TOK), 1
    )
    wide_ids = jnp.broadcast_to(ids, (TOK, TOK)).astype(F32)
    same = jnp.where((jnp.transpose(wide_ids) == wide_ids) & before, 1.0, 0.0)
    rank = jnp.sum(same, axis=0, keepdims=True)
    dz = ((ids >> 4) + 4 - z) & 3
    dy = (((ids >> 2) & 3) + 4 - y) & 3
    slab = ((dy + 4 - dz) & 3) * GROUP + dz * 2 + (((ids & 1) + core) & 1)
    row = slab * SLAB + mine * CAP
    meta[mine, 0:1, :] = side
    meta[mine, 1:2, :] = row.astype(F32) + rank
    meta[mine, 2:3, :] = p_row[...].astype(F32)
    meta[mine, 3:8, :] = jnp.zeros((5, TOK), F32)

    def m_copy(i):
        return pltpu.make_async_remote_copy(
            src_ref=meta.at[mine], dst_ref=meta.at[mine],
            send_sem=m_send.at[i], recv_sem=m_recv.at[i],
            device_id=mate(i)[3], device_id_type=MESH,
        )

    for i in (2, 1, 3):
        m_copy(i).start()
    load_g.wait()
    pack(gv, pg)
    x_near(1, pg, gr).start()

    x_near(0, px, xr).wait_recv()
    x_pass(0, xr).start()
    x_over(1, g, gr).start()

    for i in (1, 2, 3):
        m_copy(i).wait_recv()
    for m in range(4):
        want = jnp.where(meta[m, 0:1, :] == my_side, meta[m, 1:2, :], -1.0)
        prob = meta[m, 2:3, :]
        for r in range(4):
            at = lax.broadcasted_iota(jnp.int32, (ROWS, TOK), 0).astype(F32) + float(r * ROWS)
            hit = at == want
            one[r * ROWS : (r + 1) * ROWS, m * TOK : (m + 1) * TOK] = jnp.where(
                hit, 1.0, 0.0
            ).astype(BF)
            onep[r * ROWS : (r + 1) * ROWS, m * TOK : (m + 1) * TOK] = jnp.where(
                hit, prob, 0.0
            ).astype(BF)
        down = jnp.transpose(jnp.broadcast_to(want, (TOK, TOK)))
        for r in range(4 * ROWS // TOK):
            at = lax.broadcasted_iota(jnp.int32, (TOK, TOK), 1).astype(F32) + float(r * TOK)
            onet[m * TOK : (m + 1) * TOK, r * TOK : (r + 1) * TOK] = jnp.where(
                at == down, 1.0, 0.0
            ).astype(BF)

    def group_send(q, sign, src, dst, s_sem, r_sem, lanes=slice(None)):
        first = jnp.where(q == 0, 1, 0).astype(jnp.int32)

        def one_send(step, _):
            i = GROUP - 1 + first - step
            at = q * GROUP + i
            pltpu.make_async_remote_copy(
                src_ref=src.at[at, :, lanes], dst_ref=dst.at[at, :, lanes],
                send_sem=s_sem, recv_sem=r_sem,
                device_id=place_of(q, i, sign), device_id_type=MESH,
            ).start()
            return 0

        lax.fori_loop(first, GROUP, one_send, 0)

    def group_wait(count, first, src, dst, sem, lanes=slice(None)):
        pltpu.make_async_copy(
            src.at[pl.ds(first, count), :, lanes], dst.at[pl.ds(first, count), :, lanes], sem
        ).wait()

    def gather_and_send(a, turn, picks, rows, src, dst):
        @pl.loop(0, 4)
        def _(step):
            q = turn(step)

            @pl.loop(0, WIDE // TILE)
            def _(n):
                lanes = pl.ds(pl.multiple_of(n * TILE, TILE), TILE)
                here = pl.ds(pl.multiple_of(q * ROWS, ROWS), ROWS)
                got = dot(picks[here, :], rows[:, lanes], (1, 0)).astype(BF)
                src[pl.ds(q * GROUP, GROUP), :, lanes] = got.reshape(GROUP, SLAB, TILE)

            group_send(q, 1, src, dst, y_send.at[a, q], y_recv.at[a, q])

            @pl.when(q == 0)
            def _():
                pltpu.make_async_copy(src.at[0], dst.at[0], y_recv.at[a, 0]).start()

    x_near(1, pg, gr).wait_recv()
    x_pass(1, gr).start()
    x_over(0, x, xr).wait_recv()
    x_pass(0, xr).wait_recv()
    x_own(0, x, xr).wait()
    gather_and_send(0, lambda step: step, one, xr, sx, x3)

    other = (e, 1 - xl)

    def d_copy(a, q):
        src, dst = ((pgu, qgu), (pr, qr))[a]
        at = q
        return pltpu.make_async_remote_copy(
            src_ref=src.at[at], dst_ref=dst.at[at],
            send_sem=d_send.at[a, q], recv_sem=d_recv.at[a, q],
            device_id=other, device_id_type=MESH,
        )

    for i, (w, v) in enumerate(((wg, vg), (wu, vu), (wd, vd))):
        pltpu.make_async_copy(w, v, w_sem.at[i]).wait()

    def gate_and_up(q, _):
        at = q
        group_wait(GROUP, at * GROUP, sx, x3, y_recv.at[0, q])

        @pl.loop(0, HID // TILE)
        def _(n):
            lanes = pl.ds(pl.multiple_of(n * TILE, TILE), TILE)
            more = pl.ds(pl.multiple_of(HID + n * TILE, TILE), TILE)
            left = x3[pl.ds(at * GROUP, GROUP)].reshape(ROWS, WIDE)
            pgu[at, :, lanes] = dot(left, vg[0, :, lanes], (1, 0)).astype(BF)
            pgu[at, :, more] = dot(left, vu[0, :, lanes], (1, 0)).astype(BF)

        d_copy(0, q).start()
        return 0

    lax.fori_loop(0, 1, gate_and_up, 0)
    x_over(1, g, gr).wait_recv()
    x_pass(1, gr).wait_recv()
    x_own(1, g, gr).wait()
    gather_and_send(1, lambda step: step, onep, gr, sg, g3)

    lax.fori_loop(1, 4, gate_and_up, 0)

    @pl.loop(0, 4)
    def _(step):
        q = step
        at = q
        group_wait(GROUP, at * GROUP, sg, g3, y_recv.at[1, q])

        @pl.loop(0, HID // TILE)
        def _(n):
            lanes = pl.ds(pl.multiple_of(n * TILE, TILE), TILE)
            left = g3[pl.ds(at * GROUP, GROUP)].reshape(ROWS, WIDE)
            pr[at, :, lanes] = dot(left, vd[0, :, lanes], (1, 0)).astype(BF)

        d_copy(1, q).start()

    def piece(c):
        first, end = PIECES[c]
        return pl.ds(first * TILE, (end - first) * TILE + (EXTRA if c == 3 else 0))

    @pl.loop(0, 4)
    def _(step):
        q = step
        at = q
        d_copy(0, q).wait_recv()
        d_copy(1, q).wait_recv()
        here = pl.ds(pl.multiple_of(at * ROWS, ROWS), ROWS)

        def act(n, total):
            lanes = pl.ds(pl.multiple_of(n * TILE, TILE), TILE)
            more = pl.ds(pl.multiple_of(HID + n * TILE, TILE), TILE)
            gate = pgu[at, :, lanes].astype(F32) + qgu[at, :, lanes].astype(F32)
            up = pgu[at, :, more].astype(F32) + qgu[at, :, more].astype(F32)
            d = pr[at, :, lanes].astype(F32) + qr[at, :, lanes].astype(F32)
            s = jax.nn.sigmoid(gate)
            silu = gate * s
            hidden = silu * up
            rows_h[here, lanes] = hidden.astype(BF)
            rows_gu[here, lanes] = (d * up * (s * (1.0 + gate * (1.0 - s)))).astype(BF)
            rows_gu[here, more] = (d * silu).astype(BF)
            return total + jnp.sum(hidden * d, axis=1, keepdims=True)

        total = lax.fori_loop(0, HID // TILE, act, jnp.zeros((ROWS, 1), F32))
        b3[pl.ds(at * GROUP, GROUP), :, WIDE:] = (
            jnp.broadcast_to(total, (ROWS, EXTRA)).astype(BF).reshape(GROUP, SLAB, EXTRA)
        )

        @pl.loop(0, WIDE // TILE)
        def _(n):
            lanes = pl.ds(pl.multiple_of(n * TILE, TILE), TILE)
            back = dot(rows_gu[here, :HID], vg[0, lanes, :], (1, 1)) + dot(
                rows_gu[here, HID:], vu[0, lanes, :], (1, 1)
            )
            b3[pl.ds(at * GROUP, GROUP), :, lanes] = back.astype(BF).reshape(GROUP, SLAB, TILE)
            for c in range(4):

                @pl.when(n == PIECES[c][1] - 1)
                def _(c=c):
                    sems = b_send.at[q, c], b_recv.at[q, c]
                    group_send(q, -1, b3, r3, *sems, piece(c))

                    @pl.when(q == 0)
                    def _():
                        pltpu.make_async_copy(
                            b3.at[0, :, piece(c)], r3.at[0, :, piece(c)], sems[1]
                        ).start()

    def o_copy(i, c):
        _, _, m, where = mate(i)
        return pltpu.make_async_remote_copy(
            src_ref=out_s.at[m, :, piece(c)], dst_ref=out_r.at[mine, :, piece(c)],
            send_sem=o_send.at[i, c], recv_sem=o_recv.at[i, c],
            device_id=where, device_id_type=MESH,
        )

    def pick(lanes, width):
        got = dot(onet[...], r3[:, :, lanes].reshape(4 * ROWS, width), (1, 0))
        out_s[:, :, lanes] = got.astype(BF).reshape(4, TOK, width)
        out_r[mine, :, lanes] = out_s[mine, :, lanes]

    @pl.loop(0, WIDE // TILE)
    def _(n):
        for c in range(4):

            @pl.when(n == PIECES[c][0])
            def _(c=c):
                for q in (3, 2, 1, 0):
                    group_wait(GROUP, q * GROUP, b3, r3, b_recv.at[q, c], piece(c))

        pick(pl.ds(pl.multiple_of(n * TILE, TILE), TILE), TILE)
        for c in range(4):

            @pl.when(n == PIECES[c][1] - 1)
            def _(c=c):
                if c == 3:
                    pick(pl.ds(WIDE, EXTRA), EXTRA)
                for i in (2, 1, 3):
                    o_copy(i, c).start()

    @pl.loop(0, WIDE // TILE)
    def _(n):
        lanes = pl.ds(pl.multiple_of(n * TILE, TILE), TILE)
        left = g3[:, :, lanes].reshape(4 * ROWS, TILE)
        vd[0, lanes, :] = dot(left, rows_h[...], (0, 0)).astype(BF)
        left = x3[:, :, lanes].reshape(4 * ROWS, TILE)
        vg[0, lanes, :] = dot(left, rows_gu[:, :HID], (0, 0)).astype(BF)
        vu[0, lanes, :] = dot(left, rows_gu[:, HID:], (0, 0)).astype(BF)

    for c in range(4):
        for i in (1, 2, 3):
            o_copy(i, c).wait_recv()
    for k in range(2):
        dx[:, k * WIDE : (k + 1) * WIDE] = (
            out_r[k, :, :WIDE].astype(F32) + out_r[2 + k, :, :WIDE].astype(F32)
        ).astype(BF)
    term = jnp.transpose(out_r[0, :, WIDE:].astype(F32) + out_r[2, :, WIDE:].astype(F32))
    dprob[...] = (term[0:1] / p_row[...].astype(F32)).astype(BF)

    for i in (1, 2, 3):
        m_copy(i).wait_send()
        for c in range(4):
            o_copy(i, c).wait_send()
    for a, (src, packed, dst) in enumerate(((x, px, xr), (g, pg, gr))):
        x_near(a, packed, dst).wait_send()
        x_over(a, src, dst).wait_send()
        x_pass(a, dst).wait_send()
    for q in range(4):
        count = GROUP - (q == 0)
        group_wait(count, 0, sx, x3, y_send.at[0, q])
        group_wait(count, 0, sg, g3, y_send.at[1, q])
        for c in range(4):
            group_wait(count, 0, b3, r3, b_send.at[q, c], piece(c))
        d_copy(0, jnp.int32(q)).wait_send()
        d_copy(1, jnp.int32(q)).wait_send()


def place(*refs):
    count = (len(refs) - 1) // 2
    copies = [
        pltpu.make_async_copy(refs[i], refs[count + i], refs[-1].at[i]) for i in range(count)
    ]
    for copy in copies:
        copy.start()
    for copy in copies:
        copy.wait()


def on_device(activations, out_grad, expert_ids, gate_probs, gate_weight, up_weight, down_weight):
    vmem = pl.BlockSpec(memory_space=pltpu.VMEM)
    hbm = pl.BlockSpec(memory_space=pl.ANY)
    dma = pltpu.SemaphoreType.DMA
    slabs = (4 * GROUP, SLAB, WIDE)
    grad = pltpu.VMEM((1, WIDE, HID), BF)
    dx, dprob, *grads = (
        pl.pallas_call(
            kernel,
            out_shape=(
                pltpu.VMEM((TOK, 2 * WIDE), BF),
                pltpu.VMEM((1, TOK), BF),
                grad, grad, grad,
            ),
            in_specs=[vmem] * 2 + [hbm] * 5,
            out_specs=(vmem,) * 5,
            scratch_shapes=[
                pltpu.VMEM((4, 8, TOK), F32),
                pltpu.VMEM((TOK, 2 * WIDE), BF), pltpu.VMEM((TOK, 2 * WIDE), BF),
                pltpu.VMEM((TOK, WIDE), BF), pltpu.VMEM((TOK, WIDE), BF),
                pltpu.VMEM((4 * TOK, WIDE), BF),
                pltpu.VMEM((4 * TOK, WIDE), BF),
                pltpu.VMEM((4 * ROWS, 4 * TOK), BF),
                pltpu.VMEM((4 * ROWS, 4 * TOK), BF),
                pltpu.VMEM((4 * TOK, 4 * ROWS), BF),
                pltpu.VMEM(slabs, BF), pltpu.VMEM(slabs, BF),
                pltpu.VMEM(slabs, BF), pltpu.VMEM(slabs, BF),
                pltpu.VMEM((4, ROWS, 2 * HID), BF), pltpu.VMEM((4, ROWS, HID), BF),
                pltpu.VMEM((4, ROWS, 2 * HID), BF), pltpu.VMEM((4, ROWS, HID), BF),
                pltpu.VMEM((4 * ROWS, 2 * HID), BF), pltpu.VMEM((4 * ROWS, HID), BF),
                pltpu.VMEM((4 * GROUP, SLAB, WIDE + EXTRA), BF),
                pltpu.VMEM((4 * GROUP, SLAB, WIDE + EXTRA), BF),
                pltpu.VMEM((4, TOK, WIDE + EXTRA), BF),
                pltpu.VMEM((4, TOK, WIDE + EXTRA), BF),
                dma((3,)), dma((4,)), dma((4,)), dma((2, 4)), dma((2, 4)), dma((2, 4)), dma((2, 4)),
                dma((2, 4)), dma((2, 4)), dma((4, 4)), dma((4, 4)), dma((4, 4)), dma((4, 4)),
            ],
            compiler_params=pltpu.CompilerParams(
                has_side_effects=True, collective_id=0, vmem_limit_bytes=49 << 20
            ),
            cost_estimate=pl.CostEstimate(
                flops=8 * 2 * 4 * ROWS * WIDE * HID, bytes_accessed=6 * 2 * WIDE * HID, transcendentals=4 * ROWS * HID
            ),
        )(
            expert_ids.reshape(1, TOK),
            gate_probs.reshape(1, TOK),
            activations, out_grad, gate_weight, up_weight, down_weight,
        )
    )
    made = [pltpu.with_memory_space_constraint(a, pltpu.VMEM) for a in (dx, dprob, *grads)]
    dx, dprob, *grads = pl.pallas_call(
        place,
        out_shape=[jax.ShapeDtypeStruct(a.shape, a.dtype) for a in made],
        in_specs=[vmem] * 5,
        out_specs=[hbm] * 5,
        scratch_shapes=[dma((5,))],
        compiler_params=pltpu.CompilerParams(vmem_limit_bytes=1 << 20),
    )(*made)
    return dx, dprob.reshape(TOK, 1), *grads


def solution(mesh):
    rows, weights = P(("expert", "dp"), None), P("expert", "dp", None)
    return jax.shard_map(
        on_device,
        mesh=mesh,
        in_specs=(rows, rows, rows, rows, weights, weights, weights),
        out_specs=(rows, rows, weights, weights, weights),
        check_vma=False,
    )
```
